512 devices in a mesh: dp: 4 (over x), own: 128 (over z, y, core).
Axes of the slice: x: 4, y: 4, z: 16, core: 2. Of those that a mesh axis runs over, the one named last changes fastest.
Arguments:
- partial_grads: bfloat16 [4, 128, 512, 512], P('dp', None, 'own'), may hold values from -6 to 6
- owner_list: int32 [128], replicated, may hold values from 0 to 127, as said below
- left_stat: float32 [256, 512, 512], P('own', 'dp'), may hold values from -6 to 6
- right_stat: float32 [256, 512, 512], P('own', 'dp'), may hold values from -6 to 6
- left_root: bfloat16 [256, 512, 512], P('own', 'dp'), as said below
- right_root: bfloat16 [256, 512, 512], P('own', 'dp'), as said below
Outputs:
- new_left: float32 [256, 512, 512], P('own', 'dp')
- new_right: float32 [256, 512, 512], P('own', 'dp')
- update: bfloat16 [128, 512, 512], P(None, 'own', 'dp')
The draws below stay inside these ranges and needn't reach their ends.
Inputs may be any that keep to these rules, and one draw needn't show every extreme that they name: `owner_list`: each owner is named by at most 2 blocks; a quarter of the owners are named by exactly 2 blocks, half by one, a quarter by none. `left_root`: each matrix is symmetric and positive definite. `right_root`: each matrix is symmetric and positive definite.
All inputs are finite; a program needn't handle non-finite values.
Results may differ from the reference program's by a relative error of at most 0.015.
Values may be sent and summed in bfloat16 or wider, within the bound.
No kernel may reach another device: no remote copies, remote signals or barrier semaphores. Data moves between devices by JAX's collectives and lax.ppermute only.
A program may use at most 64 MiB of HBM per device.

```python
import jax
import jax.numpy as jnp
from jax import lax

BLOCK = 512
CAP = 2
NBLK = 128
SLOTS = 256
N_DP = 4
N_OWN = 128


def draw_owner_list(key, part):
    key = jax.random.fold_in(key, 11)
    first_key, second_key = jax.random.split(key)
    owner_order = jax.random.permutation(first_key, N_OWN)
    blocks = jnp.arange(NBLK, dtype=jnp.int32)
    picked = jnp.where(blocks < NBLK // 2, blocks // 2, blocks - NBLK // 4)
    raw_owner = owner_order[picked]
    shuffle = jax.random.permutation(second_key, NBLK)
    return raw_owner[shuffle].astype(jnp.int32)


def symmetric_factor(key, ramp_low, ramp_high, jitter):
    noise_key, diag_key = jax.random.split(key)
    noise = jax.random.normal(noise_key, (SLOTS, BLOCK, BLOCK), jnp.float32)
    factor = jax.random.uniform(diag_key, (SLOTS, BLOCK, 1), jnp.float32, 1.0 - jitter, 1.0 + jitter)
    position = jnp.arange(BLOCK, dtype=jnp.float32)[None, :, None] / (BLOCK - 1.0)
    diagonal = (ramp_low + (ramp_high - ramp_low) * position) * factor
    mirrored = (noise + jnp.swapaxes(noise, 1, 2)) * (0.15 / BLOCK ** 0.5)
    identity = jnp.eye(BLOCK, dtype=jnp.float32)[None, :, :]
    return mirrored + identity * diagonal


def draw_left_root(key, part):
    key = jax.random.fold_in(key, 21)
    return symmetric_factor(key, 0.75, 2.5, 0.15).astype(jnp.bfloat16)


def draw_right_root(key, part):
    key = jax.random.fold_in(key, 22)
    return symmetric_factor(key, 0.75, 2.5, 0.15).astype(jnp.bfloat16)


def level_of(stream_key, shape, cuts, least, high):
    def one(axis_at, blocks):
        steps = jax.random.uniform(jax.random.fold_in(jax.random.fold_in(stream_key, 6), axis_at), (blocks,), jnp.float32, least / len(cuts), high / len(cuts))
        return jnp.repeat(jnp.exp(steps), shape[axis_at] // blocks).reshape((-1,) + (1,) * (len(shape) - axis_at - 1))

    loudness = one(*cuts[0])
    for cut in cuts[1:]:
        loudness = loudness * one(*cut)
    return loudness


def normal_values(rng, dims, width, limit, pieces=(), held_as=jnp.bfloat16):
    values = width * jax.random.normal(rng, dims, jnp.float32)
    if pieces:
        values = values * level_of(rng, dims, pieces, -0.22, 0.18)
    return jnp.clip(values, -limit, limit).astype(held_as)


def setup_inputs(seed: int = 0) -> dict:
    splits = jax.random.split(jax.random.key(seed), 7)
    partial_grads = normal_values(splits[0], (N_DP, NBLK, BLOCK, BLOCK), 1.0, 6.0, ((0, 4), (2, 128)))
    owner_list = draw_owner_list(jax.random.fold_in(splits[6], 71), 0)
    left_stat = normal_values(splits[2], (SLOTS, BLOCK, BLOCK), 1.0, 6.0, ((0, 128), (1, 4)), jnp.float32)
    right_stat = normal_values(splits[3], (SLOTS, BLOCK, BLOCK), 1.0, 6.0, ((0, 128), (1, 4)), jnp.float32)
    left_root = draw_left_root(jax.random.fold_in(splits[6], 71), 0)
    right_root = draw_right_root(jax.random.fold_in(splits[6], 71), 0)
    return {"partial_grads": partial_grads, "owner_list": owner_list, "left_stat": left_stat, "right_stat": right_stat, "left_root": left_root, "right_root": right_root}


decay_rate = 0.95
epsilon = 1e-06

def slot_numbers(owner_list):
    owner_hits = (owner_list[:, None] == jnp.arange(N_OWN, dtype=jnp.int32)[None, :]).astype(jnp.int32)
    before = jnp.cumsum(owner_hits, axis=0) - owner_hits
    return lax.optimization_barrier(jnp.sum(before * owner_hits, axis=1)).astype(jnp.int32)

def per_slot(slot_items):
    grad_block, slot_flag, left_old, right_old, left_factor, right_factor = slot_items
    left_gram = jnp.dot(grad_block, grad_block.T, preferred_element_type=jnp.float32)
    right_gram = jnp.dot(grad_block.T, grad_block, preferred_element_type=jnp.float32)
    left_next = jnp.where(slot_flag > 0, decay_rate * left_old + left_gram / BLOCK, left_old)
    right_next = jnp.where(slot_flag > 0, decay_rate * right_old + right_gram / BLOCK, right_old)
    half_done = jnp.dot(grad_block, right_factor, preferred_element_type=jnp.float32).astype(jnp.bfloat16)
    product = jnp.dot(left_factor, half_done, preferred_element_type=jnp.float32)
    cell_count = float(BLOCK * BLOCK)
    grad_sq = jnp.sum(jnp.square(grad_block.astype(jnp.float32)))
    prod_sq = jnp.sum(product * product)
    graft_ratio = jnp.sqrt(grad_sq / cell_count) / jnp.sqrt(prod_sq / cell_count + epsilon)
    return (left_next, right_next, (product * graft_ratio).astype(jnp.bfloat16))

def reference(partial_grads, owner_list, left_stat, right_stat, left_root, right_root):
    summed_grads = lax.optimization_barrier(jnp.sum(partial_grads.astype(jnp.float32), axis=0)).astype(jnp.bfloat16)
    slot_index = slot_numbers(owner_list)
    where_to = (owner_list * CAP + slot_index).astype(jnp.int32)
    placed = jnp.zeros((SLOTS, BLOCK, BLOCK), jnp.bfloat16).at[where_to].set(summed_grads)
    slot_used = jnp.zeros((SLOTS,), jnp.float32).at[where_to].set(1.0)
    new_left, new_right, slot_updates = lax.map(per_slot, (placed, slot_used, left_stat, right_stat, left_root, right_root))
    return (new_left, new_right, slot_updates[where_to])
```

```python
import jax
import jax.numpy as jnp
from jax import lax
from jax.sharding import PartitionSpec as P

decay_rate = 0.95
epsilon = 1e-06


def spread(piece, lanes):
    copies = jnp.broadcast_to(piece[None], (lanes,) + piece.shape)
    return lax.all_to_all(copies, "dp", split_axis=0, concat_axis=0, tiled=True)


def body(partial_grads, owner_list, left_stat, right_stat, left_root, right_root):
    owners = lax.axis_size("own")
    lanes = lax.axis_size("dp")
    capacity, quarter, width = left_stat.shape
    blocks = owner_list.shape[0]
    rows = width // owners
    block_ids = jnp.arange(blocks, dtype=jnp.int32)

    terms = partial_grads[0].reshape(blocks, rows, lanes, quarter).transpose(2, 0, 1, 3)
    terms = lax.all_to_all(terms, "dp", split_axis=0, concat_axis=0, tiled=True)
    summed = jnp.sum(terms.astype(jnp.float32), axis=0).astype(jnp.bfloat16)

    same = (owner_list[:, None] == owner_list[None, :]) & (block_ids[None, :] < block_ids[:, None])
    slot_index = jnp.sum(same.astype(jnp.int32), axis=1)
    where_to = owner_list * capacity + slot_index
    cells = jnp.arange(owners * capacity, dtype=jnp.int32)
    match = where_to[None, :] == cells[:, None]
    source = jnp.sum(jnp.where(match, block_ids[None, :], 0), axis=1)
    filled = jnp.any(match, axis=1)

    picked = summed.at[source].get(mode="promise_in_bounds")
    outgoing = jnp.where(filled[:, None, None], picked, jnp.zeros_like(picked))
    outgoing = outgoing.reshape(owners, capacity, rows, quarter)
    arrived = lax.all_to_all(outgoing, "own", split_axis=0, concat_axis=0, tiled=True)
    mine = arrived.transpose(1, 0, 2, 3).reshape(capacity, width, quarter)

    left_all = spread(left_root, lanes)
    grads = spread(mine, lanes)
    grads = grads.transpose(1, 2, 0, 3).reshape(capacity, width, width)

    lane = lax.axis_index("dp")
    used = jnp.sum((owner_list == lax.axis_index("own")).astype(jnp.int32))
    slot_used = (jnp.arange(capacity, dtype=jnp.int32) < used)[:, None, None]

    half = jnp.einsum(
        "ckn,cqn->ckq", grads, right_root, preferred_element_type=jnp.float32
    ).astype(jnp.bfloat16)
    left_full = left_all.transpose(1, 0, 2, 3).reshape(capacity, width, width)
    product = jnp.einsum("cpn,cpq->cnq", left_full, half, preferred_element_type=jnp.float32)
    prod_part = jnp.sum(product * product, axis=(1, 2))
    prod_sq = jnp.sum(spread(prod_part, lanes), axis=0)

    grad_rows = lax.dynamic_slice_in_dim(grads, lane * quarter, quarter, 1)
    left_gram = jnp.einsum("cqk,cnk->cqn", grad_rows, grads, preferred_element_type=jnp.float32)
    right_gram = jnp.einsum("ckq,ckn->cqn", mine, grads, preferred_element_type=jnp.float32)
    new_left = jnp.where(slot_used, decay_rate * left_stat + left_gram / width, left_stat)
    new_right = jnp.where(slot_used, decay_rate * right_stat + right_gram / width, right_stat)

    grad_sq = jnp.sum(jnp.square(grads.astype(jnp.float32)), axis=(1, 2))
    cell_count = float(width * width)
    ratio = jnp.sqrt(grad_sq / cell_count) / jnp.sqrt(prod_sq / cell_count + epsilon)
    scaled = (product * ratio[:, None, None]).astype(jnp.bfloat16)
    scaled = scaled.reshape(capacity, owners, rows, quarter).transpose(1, 0, 2, 3)
    returned = lax.all_to_all(scaled, "own", split_axis=0, concat_axis=0, tiled=True)
    returned = returned.reshape(owners * capacity, rows, quarter)
    update = returned.at[where_to].get(mode="promise_in_bounds")
    return (new_left, new_right, update)


def solution(mesh):
    in_specs = (
        P("dp", None, "own", None),
        P(),
        P("own", "dp", None),
        P("own", "dp", None),
        P("own", "dp", None),
        P("own", "dp", None),
    )
    out_specs = (P("own", "dp", None), P("own", "dp", None), P(None, "own", "dp"))
    return jax.shard_map(body, mesh=mesh, in_specs=in_specs, out_specs=out_specs, check_vma=False)
```

```python
import jax
import jax.numpy as jnp
from jax import lax
from jax.experimental import pallas as pl
from jax.experimental.pallas import tpu as pltpu
from jax.sharding import PartitionSpec as P

decay_rate = 0.95
epsilon = 1e-06

VMEM = pl.BlockSpec(memory_space=pltpu.VMEM)
SMEM = pl.BlockSpec(memory_space=pltpu.SMEM)
ANY = pl.BlockSpec(memory_space=pl.ANY)
PARAMS = pltpu.CompilerParams(vmem_limit_bytes=40 * 1024 * 1024)

LANE_ORDER = (2, 3, 0, 1)
OWN_SHIFT = 80


def split_columns(x_ref, out_ref):
    quarter = out_ref.shape[3]
    for place in range(out_ref.shape[0]):
        lane = LANE_ORDER[place]
        out_ref[place] = x_ref[:, :, lane * quarter : (lane + 1) * quarter]


def sum_and_place(place_ref, terms_ref, out_ref):
    out_ref[...] = jnp.zeros_like(out_ref)

    def step(block, carry):
        total = terms_ref[0, block].astype(jnp.float32)
        for term in range(1, terms_ref.shape[0]):
            total += terms_ref[term, block].astype(jnp.float32)
        out_ref[place_ref[block]] = total.astype(out_ref.dtype)
        return carry

    lax.fori_loop(0, terms_ref.shape[1], step, 0, unroll=8)


def take_cells(place_ref, cells_ref, out_ref):
    def step(block, carry):
        out_ref[block] = cells_ref[place_ref[block]]
        return carry

    lax.fori_loop(0, out_ref.shape[0], step, 0, unroll=8)


def precondition(
    lane_ref, g0, g1, g2, g3, right_hbm, l0, l1, l2, l3,
    grads_ref, product_ref, squares_ref, part_ref,
    pieces, right, lefts, g_sems, r_sem, l_sems,
):
    lane = lane_ref[0]
    g_copies = [
        pltpu.make_async_copy(src, pieces.at[s], g_sems.at[s]) for s, src in enumerate((g0, g1, g2, g3))
    ]
    r_copy = pltpu.make_async_copy(right_hbm, right, r_sem)
    l_copies = [
        pltpu.make_async_copy(src, lefts.at[s], l_sems.at[s]) for s, src in enumerate((l0, l1, l2, l3))
    ]
    for copy in g_copies + [r_copy] + l_copies:
        copy.start()

    slots, width, _ = grads_ref.shape
    quarter = right.shape[1]
    pairs = pieces.shape[1]
    cut = pairs - OWN_SHIFT // 2
    upper = lax.broadcasted_iota(jnp.int32, (pairs, 8, quarter), 1) < 4
    squares = [jnp.zeros((1, quarter), jnp.float32) for _ in range(slots)]
    for s in range(4):
        g_copies[s].wait()
        first = pieces[s, :, 0].astype(jnp.float32)
        second = pieces[s, :, 1].astype(jnp.float32)
        slot0 = jnp.where(upper, first, pltpu.roll(second, 4, 1))
        slot1 = jnp.where(upper, pltpu.roll(first, 4, 1), second)
        column = pl.multiple_of(lax.rem(lane + (4 - s), 4) * quarter, quarter)
        for c, value in enumerate((slot0, slot1)):
            squares[c] += jnp.sum(value * value, axis=(0, 1))[None]
            flat = value.reshape(width, quarter).astype(jnp.bfloat16)
            grads_ref[c, pl.ds(0, width - cut * 8), pl.ds(column, quarter)] = flat[cut * 8 :]
            grads_ref[c, pl.ds(width - cut * 8, cut * 8), pl.ds(column, quarter)] = flat[: cut * 8]
    r_copy.wait()
    halves = []
    for c in range(slots):
        half = lax.dot_general(
            grads_ref[c], right[c], (((1,), (1,)), ((), ())), preferred_element_type=jnp.float32
        )
        halves.append(half.astype(jnp.bfloat16))
    parts = [jnp.zeros((1, quarter), jnp.float32) for _ in range(slots)]
    for s in range(4):
        l_copies[s].wait()
        row = pl.multiple_of(lax.rem(lane + (4 - s), 4) * quarter, quarter)
        for c in range(slots):
            block = jnp.dot(lefts[s, c], halves[c], preferred_element_type=jnp.float32)
            product_ref[c, pl.ds(row, quarter)] = block
            parts[c] += jnp.sum(block * block, axis=0, keepdims=True)
    squares_ref[...] = jnp.zeros_like(squares_ref)
    part_ref[...] = jnp.zeros_like(part_ref)
    for c in range(slots):
        squares_ref[pl.ds(c, 1)] = jnp.broadcast_to(
            jnp.sum(squares[c], axis=1, keepdims=True), (1, quarter)
        )
        total = jnp.broadcast_to(jnp.sum(parts[c], axis=1, keepdims=True), (1, quarter))
        for place in range(part_ref.shape[0]):
            part_ref[place, pl.ds(c, 1)] = total


def graft(product_ref, squares_ref, parts_ref, out_ref):
    pairs, _, _, quarter = out_ref.shape
    width = product_ref.shape[1]
    cells = float(width * width)
    cut = OWN_SHIFT // 2
    scaled = []
    for c in range(2):
        grad_sq = squares_ref[pl.ds(c, 1)]
        prod_sq = sum(parts_ref[k, pl.ds(c, 1)] for k in range(parts_ref.shape[0]))
        ratio = jnp.sqrt(grad_sq / cells) / jnp.sqrt(prod_sq / cells + epsilon)
        scaled.append((product_ref[c] * ratio).reshape(pairs, 8, quarter))
    upper = lax.broadcasted_iota(jnp.int32, (pairs, 8, quarter), 1) < 4
    first = jnp.where(upper, scaled[0], pltpu.roll(scaled[1], 4, 1)).astype(out_ref.dtype)
    second = jnp.where(upper, pltpu.roll(scaled[0], 4, 1), scaled[1]).astype(out_ref.dtype)
    for member, value in enumerate((first, second)):
        out_ref[pl.ds(0, pairs - cut), member] = value[cut:]
        out_ref[pl.ds(pairs - cut, cut), member] = value[:cut]


def lane_shift(x, step, lanes):
    return lax.ppermute(x, "dp", [(i, (i + step) % lanes) for i in range(lanes)])


def body(partial_grads, owner_list, left_stat, right_stat, left_root, right_root):
    owners = lax.axis_size("own")
    lanes = lax.axis_size("dp")
    capacity, quarter, width = left_stat.shape
    blocks = owner_list.shape[0]
    rows = width // owners
    block_ids = jnp.arange(blocks, dtype=jnp.int32)
    lane = lax.axis_index("dp")
    lane_groups = [list(LANE_ORDER)]
    own_groups = [[(i + OWN_SHIFT) % owners for i in range(owners)]]

    terms = pl.pallas_call(
        split_columns,
        out_shape=jax.ShapeDtypeStruct((lanes, blocks, rows, quarter), jnp.bfloat16),
        in_specs=[VMEM],
        out_specs=VMEM,
        compiler_params=PARAMS,
        name="split_columns",
    )(partial_grads[0])
    terms = lax.all_to_all(
        terms, "dp", split_axis=0, concat_axis=0, tiled=True, axis_index_groups=lane_groups
    )

    same = (owner_list[:, None] == owner_list[None, :]) & (block_ids[None, :] < block_ids[:, None])
    slot_index = jnp.sum(same.astype(jnp.int32), axis=1)
    place = lax.rem(owner_list + (owners - OWN_SHIFT), owners) * capacity + slot_index

    outgoing = pl.pallas_call(
        sum_and_place,
        out_shape=jax.ShapeDtypeStruct((owners * capacity, rows, quarter), jnp.bfloat16),
        in_specs=[SMEM, VMEM],
        out_specs=VMEM,
        compiler_params=PARAMS,
        name="sum_and_place",
    )(place, terms)
    outgoing = outgoing.reshape(owners, capacity * rows, quarter)
    left_mine, outgoing = lax.optimization_barrier((left_root, outgoing))
    arrived = lax.all_to_all(
        outgoing, "own", split_axis=0, concat_axis=0, tiled=True, axis_index_groups=own_groups
    )
    lefts = [left_mine] + [lane_shift(left_mine, s, lanes) for s in range(1, lanes)]

    arrived = arrived.reshape(owners // 2, 2, capacity * rows, quarter)
    pieces = [arrived] + [lane_shift(arrived, s, lanes) for s in range(1, lanes)]
    grads, product, squares, part = pl.pallas_call(
        precondition,
        out_shape=(
            jax.ShapeDtypeStruct((capacity, width, width), jnp.bfloat16),
            jax.ShapeDtypeStruct((capacity, width, quarter), jnp.float32),
            jax.ShapeDtypeStruct((8, quarter), jnp.float32),
            jax.ShapeDtypeStruct((lanes, 8, quarter), jnp.float32),
        ),
        in_specs=[SMEM] + [ANY] * 9,
        out_specs=(VMEM, VMEM, VMEM, VMEM),
        scratch_shapes=[
            pltpu.VMEM((lanes, owners // 2, 2, capacity * rows, quarter), jnp.bfloat16),
            pltpu.VMEM((capacity, quarter, width), jnp.bfloat16),
            pltpu.VMEM((lanes, capacity, quarter, width), jnp.bfloat16),
            pltpu.SemaphoreType.DMA((lanes,)),
            pltpu.SemaphoreType.DMA,
            pltpu.SemaphoreType.DMA((lanes,)),
        ],
        compiler_params=PARAMS,
        name="precondition",
    )(lane.reshape(1), *pieces, right_root, *lefts)
    parts = lax.all_to_all(
        part, "dp", split_axis=0, concat_axis=0, tiled=True, axis_index_groups=lane_groups
    )
    scaled = pl.pallas_call(
        graft,
        out_shape=jax.ShapeDtypeStruct((owners // 2, 2, capacity * rows, quarter), jnp.bfloat16),
        in_specs=[VMEM, VMEM, VMEM],
        out_specs=VMEM,
        compiler_params=PARAMS,
        name="graft",
    )(product, squares, parts)
    scaled = scaled.reshape(owners, capacity * rows, quarter)
    grads, scaled = lax.optimization_barrier((grads, scaled))
    returned = lax.all_to_all(
        scaled, "own", split_axis=0, concat_axis=0, tiled=True, axis_index_groups=own_groups
    )

    used = jnp.sum((owner_list == lax.axis_index("own")).astype(jnp.int32))
    slot_used = (jnp.arange(capacity, dtype=jnp.int32) < used)[:, None, None]
    grad_rows = lax.dynamic_slice_in_dim(grads, lane * quarter, quarter, 1)
    grad_cols = lax.dynamic_slice_in_dim(grads, lane * quarter, quarter, 2)
    left_gram = jnp.einsum("cqk,cnk->cqn", grad_rows, grads, preferred_element_type=jnp.float32)
    right_gram = jnp.einsum("ckq,ckn->cqn", grad_cols, grads, preferred_element_type=jnp.float32)
    new_left = jnp.where(slot_used, decay_rate * left_stat + left_gram / width, left_stat)
    new_right = jnp.where(slot_used, decay_rate * right_stat + right_gram / width, right_stat)

    update = pl.pallas_call(
        take_cells,
        out_shape=jax.ShapeDtypeStruct((blocks, rows, quarter), jnp.bfloat16),
        in_specs=[SMEM, VMEM],
        out_specs=VMEM,
        compiler_params=PARAMS,
        name="take_cells",
    )(place, returned.reshape(owners * capacity, rows, quarter))
    return (new_left, new_right, update)


def solution(mesh):
    in_specs = (
        P("dp", None, "own", None),
        P(),
        P("own", "dp", None),
        P("own", "dp", None),
        P("own", "dp", None),
        P("own", "dp", None),
    )
    out_specs = (P("own", "dp", None), P("own", "dp", None), P(None, "own", "dp"))
    return jax.shard_map(body, mesh=mesh, in_specs=in_specs, out_specs=out_specs, check_vma=False)
```

```python
import jax
import jax.numpy as jnp
from jax import lax
from jax.experimental import pallas as pl
from jax.experimental.pallas import tpu as pltpu
from jax.sharding import PartitionSpec as P

decay_rate = 0.95
epsilon = 1e-06

VMEM = pl.BlockSpec(memory_space=pltpu.VMEM)
SMEM = pl.BlockSpec(memory_space=pltpu.SMEM)
ANY = pl.BlockSpec(memory_space=pl.ANY)
HBM = pl.BlockSpec(memory_space=pltpu.HBM)
PARAMS = pltpu.CompilerParams(vmem_limit_bytes=40 * 1024 * 1024)

PLANES, COLUMNS, CORES, LANES = 16, 4, 2, 4
LANE_ORDER = (2, 3, 0, 1)
COLUMN_ORDER = (2, 3, 0, 1)
FIRST_PLANE = 10
PLANE_ORDER = tuple((FIRST_PLANE + i) % PLANES for i in range(PLANES))
SEATS = COLUMNS * CORES
SEAT_ORDER = tuple(y * CORES + c for y in COLUMN_ORDER for c in range(CORES))


def split_columns(x_ref, out_ref):
    quarter = out_ref.shape[3]
    for place in range(out_ref.shape[0]):
        lane = LANE_ORDER[place]
        out_ref[place] = x_ref[:, :, lane * quarter : (lane + 1) * quarter]


def sum_and_place(place_ref, terms_ref, out_ref):
    out_ref[...] = jnp.zeros_like(out_ref)

    def step(block, carry):
        total = terms_ref[0, block].astype(jnp.float32)
        for term in range(1, terms_ref.shape[0]):
            total += terms_ref[term, block].astype(jnp.float32)
        out_ref[place_ref[block]] = total.astype(out_ref.dtype)
        return carry

    lax.fori_loop(0, terms_ref.shape[1], step, 0, unroll=8)


def take_cells(place_ref, cells_ref, out_ref):
    def step(block, carry):
        out_ref[block] = cells_ref[place_ref[block]]
        return carry

    lax.fori_loop(0, out_ref.shape[0], step, 0, unroll=8)


def fan_out(x_ref, out_hbm, slots, sems):
    for slot in range(2):
        for i, seat in enumerate(SEAT_ORDER):
            for k, plane in enumerate(PLANE_ORDER):
                slots[slot, i, plane] = x_ref[k, seat, slot]
    copies = [
        pltpu.make_async_copy(slots.at[lane % 2], out_hbm.at[i], sems.at[i])
        for i, lane in enumerate(LANE_ORDER)
    ]
    for copy in copies:
        copy.start()
    for copy in copies:
        copy.wait()


def two_terms(value):
    high = value.astype(jnp.bfloat16).astype(jnp.float32)
    return high, value - high


def paired(first, second):
    upper = lax.broadcasted_iota(jnp.int32, first.shape, first.ndim - 2) < 4
    return (
        jnp.where(upper, first, pltpu.roll(second, 4, first.ndim - 2)),
        jnp.where(upper, pltpu.roll(first, 4, first.ndim - 2), second),
    )


def precondition(
    lane_ref, pieces, left_hbm, right_hbm, beside, across, opposite, grads_ref, out_ref,
    lefts, rights, sems,
):
    lane = lane_ref[0]
    parity = lax.rem(lane, 2)
    width = grads_ref.shape[0]
    quarter = left_hbm.shape[1]

    def rows_of(x):
        return pl.ds(pl.multiple_of(x * quarter, quarter), quarter)

    copies = [
        pltpu.make_async_copy(left_hbm.at[parity], lefts.at[rows_of(parity)], sems.at[0]),
        pltpu.make_async_copy(beside.at[1], lefts.at[rows_of(1 - parity)], sems.at[1]),
        pltpu.make_async_copy(right_hbm.at[parity], rights.at[rows_of(lane)], sems.at[2]),
        pltpu.make_async_copy(beside.at[0], rights.at[rows_of(lane ^ 1)], sems.at[3]),
        pltpu.make_async_copy(across, rights.at[rows_of(lane ^ 3)], sems.at[4]),
        pltpu.make_async_copy(opposite, rights.at[rows_of(lane ^ 2)], sems.at[5]),
    ]
    for copy in copies:
        copy.start()

    square = jnp.zeros((1, 1), jnp.float32)
    for i, source in enumerate(LANE_ORDER):
        even, odd = [None] * COLUMNS, [None] * COLUMNS
        for j, y in enumerate(COLUMN_ORDER):
            even[y], odd[y] = paired(
                pieces[i, j * CORES].astype(jnp.float32),
                pieces[i, j * CORES + 1].astype(jnp.float32),
            )
        value = jnp.stack([jnp.stack(even, axis=1), jnp.stack(odd, axis=1)], axis=1)
        value = value.reshape(width // 8, 8, quarter)
        sums = jnp.sum(value * value, axis=0)
        square += jnp.sum(sums, axis=(0, 1), keepdims=True)
        flat = value.reshape(width, quarter).astype(jnp.bfloat16)
        grads_ref[:, source * quarter : (source + 1) * quarter] = flat
    for copy in copies:
        copy.wait()
    half = jnp.dot(lefts[...], grads_ref[...], preferred_element_type=jnp.float32)
    product = jnp.dot(
        half.astype(jnp.bfloat16), rights[...], preferred_element_type=jnp.float32
    )
    prod_sq = jnp.sum(jnp.sum(product * product, axis=0, keepdims=True), axis=1, keepdims=True)
    rows = lax.broadcasted_iota(jnp.int32, (8, quarter), 0)
    tail = jnp.zeros((8, quarter), jnp.float32)
    for r, value in enumerate((*two_terms(prod_sq), *two_terms(square))):
        tail = jnp.where(rows == r, value, tail)
    tail = tail.astype(out_ref.dtype)
    pairs = out_ref.shape[1] - 1
    for i, target in enumerate(LANE_ORDER):
        block = product[:, target * quarter : (target + 1) * quarter]
        block = block.reshape(pairs, 2, COLUMNS, 8, quarter)
        for j, y in enumerate(COLUMN_ORDER):
            for core, value in enumerate(paired(block[:, 0, y], block[:, 1, y])):
                seat = i * SEATS + j * CORES + core
                out_ref[seat, pl.ds(0, pairs)] = value.astype(out_ref.dtype)
                out_ref[seat, pairs] = tail


def graft(x_ref, out_ref):
    quarter = out_ref.shape[3]
    pairs = x_ref.shape[1] - 1
    cells = float((LANES * quarter) ** 2)
    for j, seat in enumerate(SEAT_ORDER):
        ratios = []
        for slot in range(2):
            upper, lower = [
                x_ref[LANE_ORDER.index(2 * half + slot) * SEATS + j, pairs].astype(jnp.float32)
                for half in range(2)
            ]
            total = upper + lower
            prod_sq = total[0:1] + total[1:2]
            grad_sq = upper[2:3] + upper[3:4]
            ratios.append(jnp.sqrt(grad_sq / cells) / jnp.sqrt(prod_sq / cells + epsilon))
        for half in range(2):
            scaled = []
            for slot in range(2):
                member = LANE_ORDER.index(2 * half + slot) * SEATS + j
                value = x_ref[member, pl.ds(0, pairs)].astype(jnp.float32)
                scaled.append(value * ratios[slot])
            for odd, value in enumerate(paired(*scaled)):
                for p in range(pairs):
                    plane = half * (PLANES // 2) + 2 * p + odd
                    place = (plane - FIRST_PLANE) % PLANES
                    out_ref[place, seat] = value[p].astype(out_ref.dtype)


def gram_rows(block, side, near):
    rows = block[near, :] if side == 0 else block[:, near]
    dims = ((1 - side,), (1 - side,))
    return lax.dot_general(rows, block[...], (dims, ((), ())), preferred_element_type=jnp.float32)


def own_statistics(
    info_ref, block, left_hbm, right_hbm, new_left_hbm, new_right_hbm, sent_ref, old, new, sems
):
    lane, used = info_ref[0], info_ref[1]
    slot = lax.rem(lane, 2)
    width = block.shape[0]
    quarter = old.shape[1]
    loads = [
        pltpu.make_async_copy(src.at[slot], old.at[i], sems.at[i])
        for i, src in enumerate((left_hbm, right_hbm))
    ]
    stores = [
        pltpu.make_async_copy(new.at[i], target.at[slot], sems.at[2 + i])
        for i, target in enumerate((new_left_hbm, new_right_hbm))
    ]
    for copy in loads:
        copy.start()
    mine = pl.ds(pl.multiple_of(lane * quarter, quarter), quarter)
    theirs = pl.ds(pl.multiple_of((lane ^ 1) * quarter, quarter), quarter)
    for i in range(2):
        gram = gram_rows(block, i, mine)
        loads[i].wait()
        was = old[i]
        new[i] = jnp.where(slot < used, decay_rate * was + gram / width, was)
        stores[i].start()
    for i in range(2):
        sent_ref[i] = gram_rows(block, i, theirs).astype(sent_ref.dtype)
    for copy in stores:
        copy.wait()


def other_statistics(
    info_ref, grams_ref, left_hbm, right_hbm, _, __, new_left_hbm, new_right_hbm, old, new, sems
):
    lane, used = info_ref[0], info_ref[1]
    slot = 1 - lax.rem(lane, 2)
    width = old.shape[2]
    loads = [
        pltpu.make_async_copy(src.at[slot], old.at[i], sems.at[i])
        for i, src in enumerate((left_hbm, right_hbm))
    ]
    stores = [
        pltpu.make_async_copy(new.at[i], target.at[slot], sems.at[2 + i])
        for i, target in enumerate((new_left_hbm, new_right_hbm))
    ]
    for copy in loads:
        copy.start()
    for i in range(2):
        loads[i].wait()
        was = old[i]
        gram = grams_ref[i].astype(jnp.float32)
        new[i] = jnp.where(slot < used, decay_rate * was + gram / width, was)
        stores[i].start()
    for copy in stores:
        copy.wait()


def lane_swap(x, mask):
    return lax.ppermute(x, "dp", [(i, i ^ mask) for i in range(LANES)])


def exchange(x, axes, groups):
    return lax.all_to_all(
        x, axes, split_axis=0, concat_axis=0, tiled=True, axis_index_groups=groups
    )


def body(partial_grads, owner_list, left_stat, right_stat, left_root, right_root):
    owners = PLANES * SEATS
    capacity, quarter, width = left_stat.shape
    blocks = owner_list.shape[0]
    rows = width // owners
    block_ids = jnp.arange(blocks, dtype=jnp.int32)
    lane = lax.axis_index("dp")
    lane_groups = [list(LANE_ORDER)]
    plane_groups = [[z * SEATS + seat for z in PLANE_ORDER] for seat in range(SEATS)]
    flat_groups = [
        [x * owners + z * SEATS + seat for x in LANE_ORDER for seat in SEAT_ORDER]
        for z in range(PLANES)
    ]

    terms = pl.pallas_call(
        split_columns,
        out_shape=jax.ShapeDtypeStruct((LANES, blocks, rows, quarter), jnp.bfloat16),
        in_specs=[VMEM],
        out_specs=VMEM,
        compiler_params=PARAMS,
        name="split_columns",
    )(partial_grads[0])
    terms = exchange(terms, "dp", lane_groups)

    same = (owner_list[:, None] == owner_list[None, :]) & (block_ids[None, :] < block_ids[:, None])
    slot_index = jnp.sum(same.astype(jnp.int32), axis=1)
    turned = lax.rem(owner_list + (PLANES - FIRST_PLANE) * SEATS, owners)
    place = turned * capacity + slot_index

    outgoing = pl.pallas_call(
        sum_and_place,
        out_shape=jax.ShapeDtypeStruct((owners * capacity, rows, quarter), jnp.bfloat16),
        in_specs=[SMEM, VMEM],
        out_specs=VMEM,
        compiler_params=PARAMS,
        name="sum_and_place",
    )(place, terms)
    outgoing = outgoing.reshape(PLANES, SEATS * capacity * rows, quarter)
    parity = lane % 2
    theirs = jnp.stack([right_root, left_root])
    theirs = lax.dynamic_index_in_dim(theirs, 1 - parity, 1, keepdims=False)
    mine = lax.dynamic_index_in_dim(right_root, parity, 0, keepdims=False)
    theirs, mine, outgoing = lax.optimization_barrier((theirs, mine, outgoing))
    arrived = exchange(outgoing, "own", plane_groups)
    opposite, beside, across = lane_swap(mine, 2), lane_swap(theirs, 1), lane_swap(theirs[0], 3)
    opposite, beside, arrived = lax.optimization_barrier((opposite, beside, arrived))

    tile = capacity * rows
    copies = pl.pallas_call(
        fan_out,
        out_shape=jax.ShapeDtypeStruct((LANES, SEATS, PLANES, rows, quarter), jnp.bfloat16),
        in_specs=[VMEM],
        out_specs=HBM,
        scratch_shapes=[
            pltpu.VMEM((capacity, SEATS, PLANES, rows, quarter), jnp.bfloat16),
            pltpu.SemaphoreType.DMA((LANES,)),
        ],
        compiler_params=PARAMS,
        name="fan_out",
    )(arrived.reshape(PLANES, SEATS, capacity, rows, quarter))
    members = LANES * SEATS
    pieces = exchange(copies.reshape(members, PLANES * rows, quarter), ("dp", "own"), flat_groups)
    pieces = pieces.reshape(LANES, SEATS, PLANES // 2, 2 * rows, quarter)

    near = PLANES // 4 + 1
    grads, product = pl.pallas_call(
        precondition,
        out_shape=(
            jax.ShapeDtypeStruct((width, width), jnp.bfloat16),
            jax.ShapeDtypeStruct((members, near, tile, quarter), jnp.bfloat16),
        ),
        in_specs=[SMEM, VMEM] + [ANY] * 5,
        out_specs=(VMEM, VMEM),
        scratch_shapes=[
            pltpu.VMEM((width // 2, width), jnp.bfloat16),
            pltpu.VMEM((width, width), jnp.bfloat16),
            pltpu.SemaphoreType.DMA((6,)),
        ],
        compiler_params=PARAMS,
        name="precondition",
    )(lane.reshape(1), pieces, left_root, right_root, beside, across, opposite)
    product = exchange(product.reshape(members, near * tile, quarter), ("dp", "own"), flat_groups)

    used = jnp.sum((owner_list == lax.axis_index("own")).astype(jnp.int32))
    info = jnp.stack([lane, used])
    stat_shapes = (
        jax.ShapeDtypeStruct(left_stat.shape, jnp.float32),
        jax.ShapeDtypeStruct(right_stat.shape, jnp.float32),
    )
    stat_scratch = [
        pltpu.VMEM((2, quarter, width), jnp.float32),
        pltpu.VMEM((2, quarter, width), jnp.float32),
        pltpu.SemaphoreType.DMA((4,)),
    ]
    light = pl.CostEstimate(flops=1, bytes_accessed=1, transcendentals=0)
    new_left, new_right, grams = pl.pallas_call(
        own_statistics,
        out_shape=stat_shapes + (jax.ShapeDtypeStruct((2, quarter, width), jnp.bfloat16),),
        in_specs=[SMEM, VMEM, HBM, HBM],
        out_specs=(HBM, HBM, VMEM),
        scratch_shapes=stat_scratch,
        compiler_params=PARAMS,
        cost_estimate=light,
        name="own_statistics",
    )(info, grads, left_stat, right_stat)
    product, grams, new_left, new_right = lax.optimization_barrier(
        (product, grams, new_left, new_right)
    )
    scaled = pl.pallas_call(
        graft,
        out_shape=jax.ShapeDtypeStruct((PLANES, SEATS, tile, quarter), jnp.bfloat16),
        in_specs=[VMEM],
        out_specs=VMEM,
        compiler_params=PARAMS,
        name="graft",
    )(product.reshape(members, near, tile, quarter))
    grams, scaled = lax.optimization_barrier((grams, scaled))
    returned = exchange(scaled.reshape(PLANES, SEATS * tile, quarter), "own", plane_groups)

    new_left, new_right = pl.pallas_call(
        other_statistics,
        out_shape=stat_shapes,
        in_specs=[SMEM, VMEM, HBM, HBM, HBM, HBM],
        out_specs=(HBM, HBM),
        scratch_shapes=stat_scratch,
        input_output_aliases={4: 0, 5: 1},
        compiler_params=PARAMS,
        cost_estimate=light,
        name="other_statistics",
    )(info, lane_swap(grams, 1), left_stat, right_stat, new_left, new_right)

    update = pl.pallas_call(
        take_cells,
        out_shape=jax.ShapeDtypeStruct((blocks, rows, quarter), jnp.bfloat16),
        in_specs=[SMEM, VMEM],
        out_specs=VMEM,
        compiler_params=PARAMS,
        name="take_cells",
    )(place, returned.reshape(owners * capacity, rows, quarter))
    return (new_left, new_right, update)


def solution(mesh):
    in_specs = (
        P("dp", None, "own", None),
        P(),
        P("own", "dp", None),
        P("own", "dp", None),
        P("own", "dp", None),
        P("own", "dp", None),
    )
    out_specs = (P("own", "dp", None), P("own", "dp", None), P(None, "own", "dp"))
    return jax.shard_map(body, mesh=mesh, in_specs=in_specs, out_specs=out_specs, check_vma=False)
```

```python
import jax
import jax.numpy as jnp
from jax import lax
from jax.experimental import pallas as pl
from jax.experimental.pallas import tpu as pltpu
from jax.sharding import PartitionSpec as P

decay_rate = 0.95
epsilon = 1e-06

VMEM = pl.BlockSpec(memory_space=pltpu.VMEM)
SMEM = pl.BlockSpec(memory_space=pltpu.SMEM)
ANY = pl.BlockSpec(memory_space=pl.ANY)
HBM = pl.BlockSpec(memory_space=pltpu.HBM)
PARAMS = pltpu.CompilerParams(vmem_limit_bytes=40 * 1024 * 1024)

PLANES, COLUMNS, CORES, LANES = 16, 4, 2, 4
LANE_ORDER = (2, 3, 0, 1)
COLUMN_ORDER = (2, 3, 0, 1)
FIRST_PLANE = 10
PLANE_ORDER = tuple((FIRST_PLANE + i) % PLANES for i in range(PLANES))
SEATS = COLUMNS * CORES
SEAT_ORDER = tuple(y * CORES + c for y in COLUMN_ORDER for c in range(CORES))


def split_columns(x_hbm, out_hbm, x, out, in_sems, out_sems):
    quarter = out.shape[3]
    parts = in_sems.shape[0]
    size = x.shape[0] // parts
    arriving, leaving = [], []
    for part in range(parts):
        blocks = pl.ds(part * size, size)
        arriving.append(pltpu.make_async_copy(x_hbm.at[blocks], x.at[blocks], in_sems.at[part]))
        leaving.append(
            pltpu.make_async_copy(out.at[:, blocks], out_hbm.at[:, blocks], out_sems.at[part])
        )
        arriving[part].start()
    for part in range(parts):
        arriving[part].wait()
        blocks = pl.ds(part * size, size)
        for place, lane in enumerate(LANE_ORDER):
            out[place, blocks] = x[blocks, :, lane * quarter : (lane + 1) * quarter]
        leaving[part].start()
    for copy in leaving:
        copy.wait()


def sum_and_place(place_ref, terms_ref, out_ref):
    out_ref[...] = jnp.zeros_like(out_ref)

    def step(block, carry):
        total = terms_ref[0, block].astype(jnp.float32)
        for term in range(1, terms_ref.shape[0]):
            total += terms_ref[term, block].astype(jnp.float32)
        out_ref[place_ref[block]] = total.astype(out_ref.dtype)
        return carry

    lax.fori_loop(0, terms_ref.shape[1], step, 0, unroll=8)


def take_cells(place_ref, cells_ref, out_ref):
    def step(block, carry):
        out_ref[block] = cells_ref[place_ref[block]]
        return carry

    lax.fori_loop(0, out_ref.shape[0], step, 0, unroll=8)


def fan_out(x_ref, out_hbm, slots, sems):
    for slot in range(2):
        for i, seat in enumerate(SEAT_ORDER):
            for k, plane in enumerate(PLANE_ORDER):
                slots[slot, i, plane] = x_ref[k, seat, slot]
    copies = [
        pltpu.make_async_copy(slots.at[lane % 2], out_hbm.at[i], sems.at[i])
        for i, lane in enumerate(LANE_ORDER)
    ]
    for copy in copies:
        copy.start()
    for copy in copies:
        copy.wait()


def two_terms(value):
    high = value.astype(jnp.bfloat16).astype(jnp.float32)
    return high, jnp.where(high < jnp.inf, value - high, 0.0)


def paired(first, second):
    upper = lax.broadcasted_iota(jnp.int32, first.shape, first.ndim - 2) < 4
    return (
        jnp.where(upper, first, pltpu.roll(second, 4, first.ndim - 2)),
        jnp.where(upper, pltpu.roll(first, 4, first.ndim - 2), second),
    )


def gram_rows(block, side, near):
    rows = block[near, :] if side == 0 else block[:, near]
    dims = ((1 - side,), (1 - side,))
    return lax.dot_general(rows, block[...], (dims, ((), ())), preferred_element_type=jnp.float32)


def pick_blocks(lane_ref, left_ref, right_ref, beside_ref, across_ref, opposite_ref):
    lane = lane_ref[0]
    parity = lax.rem(lane, 2)
    quarter = left_ref.shape[1]

    def block(ref, slot, lane_of_columns):
        columns = pl.ds(pl.multiple_of(lane_of_columns * quarter, quarter), quarter)
        return ref[slot, :, columns]

    for i, column in enumerate((lane, lane ^ 3, lane ^ 1)):
        opposite_ref[i] = block(right_ref, parity, column)
    for i, column in enumerate((lane, lane ^ 3, lane ^ 2)):
        beside_ref[i] = block(left_ref, 1 - parity, column)
    beside_ref[3] = block(right_ref, 1 - parity, lane)
    beside_ref[4] = block(right_ref, 1 - parity, lane ^ 2)
    across_ref[0] = block(right_ref, 1 - parity, lane)


def precondition(
    lane_ref, pieces, left_hbm, right_hbm, beside, across, opposite, grads_ref, out_ref, grams_ref,
    lefts, rights, sems,
):
    lane = lane_ref[0]
    parity = lax.rem(lane, 2)
    width = grads_ref.shape[0]
    quarter = left_hbm.shape[1]

    def rows_of(x):
        return pl.ds(pl.multiple_of(x * quarter, quarter), quarter)

    copies = [
        pltpu.make_async_copy(left_hbm.at[parity], lefts.at[rows_of(parity)], sems.at[0]),
        pltpu.make_async_copy(right_hbm.at[parity], rights.at[rows_of(lane)], sems.at[1]),
    ]
    for copy in copies:
        copy.start()

    square = jnp.zeros((1, 1), jnp.float32)
    for i, source in enumerate(LANE_ORDER):
        even, odd = [None] * COLUMNS, [None] * COLUMNS
        for j, y in enumerate(COLUMN_ORDER):
            even[y], odd[y] = paired(
                pieces[i, j * CORES].astype(jnp.float32),
                pieces[i, j * CORES + 1].astype(jnp.float32),
            )
        value = jnp.stack([jnp.stack(even, axis=1), jnp.stack(odd, axis=1)], axis=1)
        value = value.reshape(width // 8, 8, quarter)
        sums = jnp.sum(value * value, axis=0)
        square += jnp.sum(sums, axis=(0, 1), keepdims=True)
        flat = value.reshape(width, quarter).astype(jnp.bfloat16)
        grads_ref[:, source * quarter : (source + 1) * quarter] = flat
    for copy in copies:
        copy.wait()
    side, far, last = lane ^ 1, lane ^ 3, lane ^ 2

    def put(row, column, block):
        rights[rows_of(row), rows_of(column)] = block
        if row is not column:
            rights[rows_of(column), rows_of(row)] = block.T

    for other in (side, far, last):
        rights[rows_of(other), rows_of(lane)] = rights[rows_of(lane), rows_of(other)].T
    put(last, last, opposite[0])
    put(last, side, opposite[1])
    put(last, far, opposite[2])
    put(side, side, beside[3])
    put(side, far, beside[4])
    put(far, far, across[0])
    below = rows_of(1 - parity)
    lefts[below, rows_of(lane)] = lefts[rows_of(parity), rows_of(side)].T
    for i, column in enumerate((side, last, far)):
        lefts[below, rows_of(column)] = beside[i]
    half = jnp.dot(lefts[...], grads_ref[...], preferred_element_type=jnp.float32)
    product = jnp.dot(
        half.astype(jnp.bfloat16), rights[...], preferred_element_type=jnp.float32
    )
    prod_sq = jnp.sum(jnp.sum(product * product, axis=0, keepdims=True), axis=1, keepdims=True)
    rows = lax.broadcasted_iota(jnp.int32, (8, quarter), 0)
    tail = jnp.zeros((8, quarter), jnp.float32)
    for r, value in enumerate((*two_terms(prod_sq), *two_terms(square))):
        tail = jnp.where(rows == r, value, tail)
    tail = tail.astype(out_ref.dtype)
    pairs = out_ref.shape[1] - 1
    for i, target in enumerate(LANE_ORDER):
        block = product[:, target * quarter : (target + 1) * quarter]
        block = block.reshape(pairs, 2, COLUMNS, 8, quarter)
        for j, y in enumerate(COLUMN_ORDER):
            for core, value in enumerate(paired(block[:, 0, y], block[:, 1, y])):
                seat = i * SEATS + j * CORES + core
                out_ref[seat, pl.ds(0, pairs)] = value.astype(out_ref.dtype)
                out_ref[seat, pairs] = tail
    for side in range(2):
        grams_ref[side] = gram_rows(grads_ref, side, rows_of(lane ^ 1)).astype(grams_ref.dtype)


def graft(x_ref, out_ref):
    quarter = out_ref.shape[3]
    pairs = x_ref.shape[1] - 1
    cells = float((LANES * quarter) ** 2)
    for j, seat in enumerate(SEAT_ORDER):
        ratios = []
        for slot in range(2):
            upper, lower = [
                x_ref[LANE_ORDER.index(2 * half + slot) * SEATS + j, pairs].astype(jnp.float32)
                for half in range(2)
            ]
            total = upper + lower
            prod_sq = total[0:1] + total[1:2]
            grad_sq = upper[2:3] + upper[3:4]
            ratios.append(jnp.sqrt(grad_sq / cells) / jnp.sqrt(prod_sq / cells + epsilon))
        for half in range(2):
            scaled = []
            for slot in range(2):
                member = LANE_ORDER.index(2 * half + slot) * SEATS + j
                value = x_ref[member, pl.ds(0, pairs)].astype(jnp.float32)
                scaled.append(value * ratios[slot])
            for odd, value in enumerate(paired(*scaled)):
                for p in range(pairs):
                    plane = half * (PLANES // 2) + 2 * p + odd
                    place = (plane - FIRST_PLANE) % PLANES
                    out_ref[place, seat] = value[p].astype(out_ref.dtype)


def statistics(
    info_ref, block, grams_ref, left_hbm, right_hbm, new_left_hbm, new_right_hbm, old, new, sems
):
    lane, used = info_ref[0], info_ref[1]
    parity = lax.rem(lane, 2)
    slots = (parity, 1 - parity)
    width = block.shape[0]
    quarter = old.shape[2]
    loads, stores = [], []
    for i, slot in enumerate(slots):
        for side, (src, target) in enumerate(((left_hbm, new_left_hbm), (right_hbm, new_right_hbm))):
            loads.append(pltpu.make_async_copy(src.at[slot], old.at[i, side], sems.at[0, i, side]))
            stores.append(pltpu.make_async_copy(new.at[i, side], target.at[slot], sems.at[1, i, side]))
    for copy in loads:
        copy.start()
    mine = pl.ds(pl.multiple_of(lane * quarter, quarter), quarter)
    for i, slot in enumerate(slots):
        for side in range(2):
            if i == 0:
                gram = gram_rows(block, side, mine)
            else:
                gram = grams_ref[side].astype(jnp.float32)
            loads[2 * i + side].wait()
            was = old[i, side]
            new[i, side] = jnp.where(slot < used, decay_rate * was + gram / width, was)
            stores[2 * i + side].start()
    for copy in stores:
        copy.wait()


def lane_swap(x, mask):
    return lax.ppermute(x, "dp", [(i, i ^ mask) for i in range(LANES)])


def exchange(x, axes, groups):
    return lax.all_to_all(
        x, axes, split_axis=0, concat_axis=0, tiled=True, axis_index_groups=groups
    )


def body(partial_grads, owner_list, left_stat, right_stat, left_root, right_root):
    owners = PLANES * SEATS
    capacity, quarter, width = left_stat.shape
    blocks = owner_list.shape[0]
    rows = width // owners
    block_ids = jnp.arange(blocks, dtype=jnp.int32)
    lane = lax.axis_index("dp")
    lane_groups = [list(LANE_ORDER)]
    plane_groups = [[z * SEATS + seat for z in PLANE_ORDER] for seat in range(SEATS)]
    flat_groups = [
        [x * owners + z * SEATS + seat for x in LANE_ORDER for seat in SEAT_ORDER]
        for z in range(PLANES)
    ]

    terms = pl.pallas_call(
        split_columns,
        out_shape=jax.ShapeDtypeStruct((LANES, blocks, rows, quarter), jnp.bfloat16),
        in_specs=[HBM],
        out_specs=HBM,
        scratch_shapes=[
            pltpu.VMEM((blocks, rows, width), jnp.bfloat16),
            pltpu.VMEM((LANES, blocks, rows, quarter), jnp.bfloat16),
            pltpu.SemaphoreType.DMA((4,)),
            pltpu.SemaphoreType.DMA((4,)),
        ],
        name="split_columns",
    )(partial_grads[0])
    left, right, terms = lax.optimization_barrier((left_root, right_root, terms))
    terms = exchange(terms, "dp", lane_groups)
    picked = pl.pallas_call(
        pick_blocks,
        out_shape=[jax.ShapeDtypeStruct((n, quarter, quarter), jnp.bfloat16) for n in (5, 1, 3)],
        in_specs=[SMEM, VMEM, VMEM],
        out_specs=[VMEM] * 3,
        compiler_params=PARAMS,
        cost_estimate=pl.CostEstimate(flops=1, bytes_accessed=4 * 1024 * 1024, transcendentals=0),
        name="pick_blocks",
    )(lane.reshape(1), left, right)

    across = lane_swap(picked[1], 3)
    across, terms = lax.optimization_barrier((across, terms))

    same = (owner_list[:, None] == owner_list[None, :]) & (block_ids[None, :] < block_ids[:, None])
    slot_index = jnp.sum(same.astype(jnp.int32), axis=1)
    turned = lax.rem(owner_list + (PLANES - FIRST_PLANE) * SEATS, owners)
    place = turned * capacity + slot_index

    outgoing = pl.pallas_call(
        sum_and_place,
        out_shape=jax.ShapeDtypeStruct((owners * capacity, rows, quarter), jnp.bfloat16),
        in_specs=[SMEM, VMEM],
        out_specs=VMEM,
        compiler_params=PARAMS,
        name="sum_and_place",
    )(place, terms)
    outgoing = outgoing.reshape(PLANES, SEATS * capacity * rows, quarter)
    picked, outgoing = lax.optimization_barrier((picked, outgoing))
    arrived = exchange(outgoing, "own", plane_groups)
    beside, opposite = lane_swap(picked[0], 1), lane_swap(picked[2], 2)
    beside, opposite, arrived = lax.optimization_barrier((beside, opposite, arrived))

    tile = capacity * rows
    copies = pl.pallas_call(
        fan_out,
        out_shape=jax.ShapeDtypeStruct((LANES, SEATS, PLANES, rows, quarter), jnp.bfloat16),
        in_specs=[VMEM],
        out_specs=HBM,
        scratch_shapes=[
            pltpu.VMEM((capacity, SEATS, PLANES, rows, quarter), jnp.bfloat16),
            pltpu.SemaphoreType.DMA((LANES,)),
        ],
        compiler_params=PARAMS,
        name="fan_out",
    )(arrived.reshape(PLANES, SEATS, capacity, rows, quarter))
    members = LANES * SEATS
    pieces = exchange(copies.reshape(members, PLANES * rows, quarter), ("dp", "own"), flat_groups)
    pieces = pieces.reshape(LANES, SEATS, PLANES // 2, 2 * rows, quarter)

    near = PLANES // 4 + 1
    grads, product, grams = pl.pallas_call(
        precondition,
        out_shape=(
            jax.ShapeDtypeStruct((width, width), jnp.bfloat16),
            jax.ShapeDtypeStruct((members, near, tile, quarter), jnp.bfloat16),
            jax.ShapeDtypeStruct((2, quarter, width), jnp.bfloat16),
        ),
        in_specs=[SMEM, VMEM, ANY, ANY, VMEM, VMEM, VMEM],
        out_specs=(VMEM, VMEM, VMEM),
        scratch_shapes=[
            pltpu.VMEM((width // 2, width), jnp.bfloat16),
            pltpu.VMEM((width, width), jnp.bfloat16),
            pltpu.SemaphoreType.DMA((2,)),
        ],
        compiler_params=PARAMS,
        name="precondition",
    )(lane.reshape(1), pieces, left_root, right_root, beside, across, opposite)
    product = exchange(product.reshape(members, near * tile, quarter), ("dp", "own"), flat_groups)

    scaled = pl.pallas_call(
        graft,
        out_shape=jax.ShapeDtypeStruct((PLANES, SEATS, tile, quarter), jnp.bfloat16),
        in_specs=[VMEM],
        out_specs=VMEM,
        compiler_params=PARAMS,
        name="graft",
    )(product.reshape(members, near, tile, quarter))
    grads, grams, scaled = lax.optimization_barrier((grads, grams, scaled))
    returned = exchange(scaled.reshape(PLANES, SEATS * tile, quarter), "own", plane_groups)

    used = jnp.sum((owner_list == lax.axis_index("own")).astype(jnp.int32))
    new_left, new_right = pl.pallas_call(
        statistics,
        out_shape=(
            jax.ShapeDtypeStruct(left_stat.shape, jnp.float32),
            jax.ShapeDtypeStruct(right_stat.shape, jnp.float32),
        ),
        in_specs=[SMEM, VMEM, VMEM, HBM, HBM],
        out_specs=(HBM, HBM),
        scratch_shapes=[
            pltpu.VMEM((2, 2, quarter, width), jnp.float32),
            pltpu.VMEM((2, 2, quarter, width), jnp.float32),
            pltpu.SemaphoreType.DMA((2, 2, 2)),
        ],
        compiler_params=PARAMS,
        cost_estimate=pl.CostEstimate(flops=1, bytes_accessed=1, transcendentals=0),
        name="statistics",
    )(jnp.stack([lane, used]), grads, lane_swap(grams, 1), left_stat, right_stat)

    update = pl.pallas_call(
        take_cells,
        out_shape=jax.ShapeDtypeStruct((blocks, rows, quarter), jnp.bfloat16),
        in_specs=[SMEM, VMEM],
        out_specs=VMEM,
        compiler_params=PARAMS,
        name="take_cells",
    )(place, returned.reshape(owners * capacity, rows, quarter))
    return (new_left, new_right, update)


def solution(mesh):
    in_specs = (
        P("dp", None, "own", None),
        P(),
        P("own", "dp", None),
        P("own", "dp", None),
        P("own", "dp", None),
        P("own", "dp", None),
    )
    out_specs = (P("own", "dp", None), P("own", "dp", None), P(None, "own", "dp"))
    return jax.shard_map(body, mesh=mesh, in_specs=in_specs, out_specs=out_specs, check_vma=False)
```

```python
import jax
import jax.numpy as jnp
from jax import lax
from jax.experimental import pallas as pl
from jax.experimental.pallas import tpu as pltpu
from jax.sharding import PartitionSpec as P

decay_rate = 0.95
epsilon = 1e-06

VMEM = pl.BlockSpec(memory_space=pltpu.VMEM)
SMEM = pl.BlockSpec(memory_space=pltpu.SMEM)
ANY = pl.BlockSpec(memory_space=pl.ANY)
HBM = pl.BlockSpec(memory_space=pltpu.HBM)
PARAMS = pltpu.CompilerParams(vmem_limit_bytes=40 * 1024 * 1024)

PLANES, COLUMNS, CORES, LANES = 16, 4, 2, 4
LANE_ORDER = (2, 3, 0, 1)
COLUMN_ORDER = (2, 3, 0, 1)
FIRST_PLANE = 10
PLANE_ORDER = tuple((FIRST_PLANE + i) % PLANES for i in range(PLANES))
SEATS = COLUMNS * CORES
SEAT_ORDER = tuple(y * CORES + c for y in COLUMN_ORDER for c in range(CORES))


def split_columns(x_hbm, out_hbm, x, out, in_sems, out_sems):
    quarter = out.shape[3]
    parts = in_sems.shape[0]
    size = x.shape[0] // parts
    arriving, leaving = [], []
    for part in range(parts):
        blocks = pl.ds(part * size, size)
        arriving.append(pltpu.make_async_copy(x_hbm.at[blocks], x.at[blocks], in_sems.at[part]))
        leaving.append(
            pltpu.make_async_copy(out.at[:, blocks], out_hbm.at[:, blocks], out_sems.at[part])
        )
        arriving[part].start()
    for part in range(parts):
        arriving[part].wait()
        blocks = pl.ds(part * size, size)
        for place, lane in enumerate(LANE_ORDER):
            out[place, blocks] = x[blocks, :, lane * quarter : (lane + 1) * quarter]
        leaving[part].start()
    for copy in leaving:
        copy.wait()


def sum_and_place(place_ref, terms_ref, out_ref):
    out_ref[...] = jnp.zeros_like(out_ref)

    def step(block, carry):
        total = terms_ref[0, block].astype(jnp.float32)
        for term in range(1, terms_ref.shape[0]):
            total += terms_ref[term, block].astype(jnp.float32)
        out_ref[place_ref[block]] = total.astype(out_ref.dtype)
        return carry

    lax.fori_loop(0, terms_ref.shape[1], step, 0, unroll=8)


def take_cells(place_ref, cells_ref, out_ref):
    def step(block, carry):
        out_ref[block] = cells_ref[place_ref[block]]
        return carry

    lax.fori_loop(0, out_ref.shape[0], step, 0, unroll=8)


def fan_out(x_ref, out_hbm, slots, sems):
    for slot in range(2):
        for i, seat in enumerate(SEAT_ORDER):
            for k, plane in enumerate(PLANE_ORDER):
                slots[slot, i, plane] = x_ref[k, seat, slot]
    copies = [
        pltpu.make_async_copy(slots.at[lane % 2], out_hbm.at[i], sems.at[i])
        for i, lane in enumerate(LANE_ORDER)
    ]
    for copy in copies:
        copy.start()
    for copy in copies:
        copy.wait()


def two_terms(value):
    high = value.astype(jnp.bfloat16).astype(jnp.float32)
    return high, jnp.where(high < jnp.inf, value - high, 0.0)


def paired(first, second):
    upper = lax.broadcasted_iota(jnp.int32, first.shape, first.ndim - 2) < 4
    return (
        jnp.where(upper, first, pltpu.roll(second, 4, first.ndim - 2)),
        jnp.where(upper, pltpu.roll(first, 4, first.ndim - 2), second),
    )


def gram_rows(block, side, near):
    rows = block[near, :] if side == 0 else block[:, near]
    dims = ((1 - side,), (1 - side,))
    return lax.dot_general(rows, block[...], (dims, ((), ())), preferred_element_type=jnp.float32)


def pick_blocks(lane_ref, left_ref, right_ref, beside_ref, across_ref, opposite_ref):
    lane = lane_ref[0]
    parity = lax.rem(lane, 2)
    quarter = left_ref.shape[1]

    def block(ref, slot, lane_of_columns):
        columns = pl.ds(pl.multiple_of(lane_of_columns * quarter, quarter), quarter)
        return ref[slot, :, columns]

    for i, column in enumerate((lane, lane ^ 3, lane ^ 2)):
        beside_ref[i] = block(right_ref, 1 - parity, column)
        beside_ref[3 + i] = block(left_ref, 1 - parity, column)
    across_ref[0] = block(right_ref, 1 - parity, lane)
    across_ref[1] = block(right_ref, 1 - parity, lane ^ 1)
    opposite_ref[0] = block(right_ref, parity, lane)


def precondition(
    lane_ref, pieces, left_hbm, right_hbm, beside, across, opposite, grads_ref, out_ref, grams_ref,
    lefts, rights, sems,
):
    lane = lane_ref[0]
    parity = lax.rem(lane, 2)
    width = grads_ref.shape[0]
    quarter = left_hbm.shape[1]

    def rows_of(x):
        return pl.ds(pl.multiple_of(x * quarter, quarter), quarter)

    copies = [
        pltpu.make_async_copy(left_hbm.at[parity], lefts.at[rows_of(parity)], sems.at[0]),
        pltpu.make_async_copy(right_hbm.at[parity], rights.at[rows_of(lane)], sems.at[1]),
    ]
    for copy in copies:
        copy.start()

    square = jnp.zeros((1, 1), jnp.float32)
    for i, source in enumerate(LANE_ORDER):
        even, odd = [None] * COLUMNS, [None] * COLUMNS
        for j, y in enumerate(COLUMN_ORDER):
            even[y], odd[y] = paired(
                pieces[i, j * CORES].astype(jnp.float32),
                pieces[i, j * CORES + 1].astype(jnp.float32),
            )
        value = jnp.stack([jnp.stack(even, axis=1), jnp.stack(odd, axis=1)], axis=1)
        value = value.reshape(width // 8, 8, quarter)
        sums = jnp.sum(value * value, axis=0)
        square += jnp.sum(sums, axis=(0, 1), keepdims=True)
        flat = value.reshape(width, quarter).astype(jnp.bfloat16)
        grads_ref[:, source * quarter : (source + 1) * quarter] = flat
    for copy in copies:
        copy.wait()
    side, far, last = lane ^ 1, lane ^ 3, lane ^ 2

    def put(row, column, block):
        rights[rows_of(row), rows_of(column)] = block
        if row is not column:
            rights[rows_of(column), rows_of(row)] = block.T

    for other in (side, far, last):
        rights[rows_of(other), rows_of(lane)] = rights[rows_of(lane), rows_of(other)].T
    put(side, side, beside[0])
    put(side, last, beside[1])
    put(side, far, beside[2])
    put(far, far, across[0])
    put(far, last, across[1])
    put(last, last, opposite[0])
    below = rows_of(1 - parity)
    lefts[below, rows_of(lane)] = lefts[rows_of(parity), rows_of(side)].T
    for i, column in enumerate((side, last, far)):
        lefts[below, rows_of(column)] = beside[3 + i]
    half = jnp.dot(lefts[...], grads_ref[...], preferred_element_type=jnp.float32)
    product = jnp.dot(
        half.astype(jnp.bfloat16), rights[...], preferred_element_type=jnp.float32
    )
    prod_sq = jnp.sum(jnp.sum(product * product, axis=0, keepdims=True), axis=1, keepdims=True)
    rows = lax.broadcasted_iota(jnp.int32, (8, quarter), 0)
    tail = jnp.zeros((8, quarter), jnp.float32)
    for r, value in enumerate((*two_terms(prod_sq), *two_terms(square))):
        tail = jnp.where(rows == r, value, tail)
    tail = tail.astype(out_ref.dtype)
    pairs = out_ref.shape[1] - 1
    for i, target in enumerate(LANE_ORDER):
        block = product[:, target * quarter : (target + 1) * quarter]
        block = block.reshape(pairs, 2, COLUMNS, 8, quarter)
        for j, y in enumerate(COLUMN_ORDER):
            for core, value in enumerate(paired(block[:, 0, y], block[:, 1, y])):
                seat = i * SEATS + j * CORES + core
                out_ref[seat, pl.ds(0, pairs)] = value.astype(out_ref.dtype)
                out_ref[seat, pairs] = tail
    for side in range(2):
        grams_ref[side] = gram_rows(grads_ref, side, rows_of(lane ^ 1)).astype(grams_ref.dtype)


def graft(x_ref, out_ref):
    quarter = out_ref.shape[3]
    pairs = x_ref.shape[1] - 1
    cells = float((LANES * quarter) ** 2)
    for j, seat in enumerate(SEAT_ORDER):
        ratios = []
        for slot in range(2):
            upper, lower = [
                x_ref[LANE_ORDER.index(2 * half + slot) * SEATS + j, pairs].astype(jnp.float32)
                for half in range(2)
            ]
            total = upper + lower
            prod_sq = total[0:1] + total[1:2]
            grad_sq = upper[2:3] + upper[3:4]
            ratios.append(jnp.sqrt(grad_sq / cells) / jnp.sqrt(prod_sq / cells + epsilon))
        for half in range(2):
            scaled = []
            for slot in range(2):
                member = LANE_ORDER.index(2 * half + slot) * SEATS + j
                value = x_ref[member, pl.ds(0, pairs)].astype(jnp.float32)
                scaled.append(value * ratios[slot])
            for odd, value in enumerate(paired(*scaled)):
                for p in range(pairs):
                    plane = half * (PLANES // 2) + 2 * p + odd
                    place = (plane - FIRST_PLANE) % PLANES
                    out_ref[place, seat] = value[p].astype(out_ref.dtype)


def statistics(
    info_ref, block, grams_ref, left_hbm, right_hbm, new_left_hbm, new_right_hbm, old, new, sems
):
    lane, used = info_ref[0], info_ref[1]
    parity = lax.rem(lane, 2)
    slots = (parity, 1 - parity)
    width = block.shape[0]
    quarter = old.shape[2]
    loads, stores = [], []
    for i, slot in enumerate(slots):
        for side, (src, target) in enumerate(((left_hbm, new_left_hbm), (right_hbm, new_right_hbm))):
            loads.append(pltpu.make_async_copy(src.at[slot], old.at[i, side], sems.at[0, i, side]))
            stores.append(pltpu.make_async_copy(new.at[i, side], target.at[slot], sems.at[1, i, side]))
    for copy in loads:
        copy.start()
    mine = pl.ds(pl.multiple_of(lane * quarter, quarter), quarter)
    for i, slot in enumerate(slots):
        for side in range(2):
            if i == 0:
                gram = gram_rows(block, side, mine)
            else:
                gram = grams_ref[side].astype(jnp.float32)
            loads[2 * i + side].wait()
            was = old[i, side]
            new[i, side] = jnp.where(slot < used, decay_rate * was + gram / width, was)
            stores[2 * i + side].start()
    for copy in stores:
        copy.wait()


def lane_swap(x, mask):
    return lax.ppermute(x, "dp", [(i, i ^ mask) for i in range(LANES)])


def exchange(x, axes, groups):
    return lax.all_to_all(
        x, axes, split_axis=0, concat_axis=0, tiled=True, axis_index_groups=groups
    )


def body(partial_grads, owner_list, left_stat, right_stat, left_root, right_root):
    owners = PLANES * SEATS
    capacity, quarter, width = left_stat.shape
    blocks = owner_list.shape[0]
    rows = width // owners
    block_ids = jnp.arange(blocks, dtype=jnp.int32)
    lane = lax.axis_index("dp")
    lane_groups = [list(LANE_ORDER)]
    plane_groups = [[z * SEATS + seat for z in PLANE_ORDER] for seat in range(SEATS)]
    flat_groups = [
        [x * owners + z * SEATS + seat for x in LANE_ORDER for seat in SEAT_ORDER]
        for z in range(PLANES)
    ]

    terms = pl.pallas_call(
        split_columns,
        out_shape=jax.ShapeDtypeStruct((LANES, blocks, rows, quarter), jnp.bfloat16),
        in_specs=[HBM],
        out_specs=HBM,
        scratch_shapes=[
            pltpu.VMEM((blocks, rows, width), jnp.bfloat16),
            pltpu.VMEM((LANES, blocks, rows, quarter), jnp.bfloat16),
            pltpu.SemaphoreType.DMA((4,)),
            pltpu.SemaphoreType.DMA((4,)),
        ],
        name="split_columns",
    )(partial_grads[0])
    left, right, terms = lax.optimization_barrier((left_root, right_root, terms))
    terms = exchange(terms, "dp", lane_groups)
    picked = pl.pallas_call(
        pick_blocks,
        out_shape=[jax.ShapeDtypeStruct((n, quarter, quarter), jnp.bfloat16) for n in (6, 2, 1)],
        in_specs=[SMEM, VMEM, VMEM],
        out_specs=[VMEM] * 3,
        compiler_params=PARAMS,
        cost_estimate=pl.CostEstimate(flops=1, bytes_accessed=4 * 1024 * 1024, transcendentals=0),
        name="pick_blocks",
    )(lane.reshape(1), left, right)

    opposite = lane_swap(picked[2], 2)

    same = (owner_list[:, None] == owner_list[None, :]) & (block_ids[None, :] < block_ids[:, None])
    slot_index = jnp.sum(same.astype(jnp.int32), axis=1)
    turned = lax.rem(owner_list + (PLANES - FIRST_PLANE) * SEATS, owners)
    place = turned * capacity + slot_index

    outgoing = pl.pallas_call(
        sum_and_place,
        out_shape=jax.ShapeDtypeStruct((owners * capacity, rows, quarter), jnp.bfloat16),
        in_specs=[SMEM, VMEM],
        out_specs=VMEM,
        compiler_params=PARAMS,
        name="sum_and_place",
    )(place, terms)
    outgoing = outgoing.reshape(PLANES, SEATS * capacity * rows, quarter)
    picked, opposite, outgoing = lax.optimization_barrier((picked, opposite, outgoing))
    arrived = exchange(outgoing, "own", plane_groups)
    beside, across = lane_swap(picked[0], 1), lane_swap(picked[1], 3)
    beside, across, arrived = lax.optimization_barrier((beside, across, arrived))

    tile = capacity * rows
    copies = pl.pallas_call(
        fan_out,
        out_shape=jax.ShapeDtypeStruct((LANES, SEATS, PLANES, rows, quarter), jnp.bfloat16),
        in_specs=[VMEM],
        out_specs=HBM,
        scratch_shapes=[
            pltpu.VMEM((capacity, SEATS, PLANES, rows, quarter), jnp.bfloat16),
            pltpu.SemaphoreType.DMA((LANES,)),
        ],
        compiler_params=PARAMS,
        name="fan_out",
    )(arrived.reshape(PLANES, SEATS, capacity, rows, quarter))
    members = LANES * SEATS
    pieces = exchange(copies.reshape(members, PLANES * rows, quarter), ("dp", "own"), flat_groups)
    pieces = pieces.reshape(LANES, SEATS, PLANES // 2, 2 * rows, quarter)

    near = PLANES // 4 + 1
    grads, product, grams = pl.pallas_call(
        precondition,
        out_shape=(
            jax.ShapeDtypeStruct((width, width), jnp.bfloat16),
            jax.ShapeDtypeStruct((members, near, tile, quarter), jnp.bfloat16),
            jax.ShapeDtypeStruct((2, quarter, width), jnp.bfloat16),
        ),
        in_specs=[SMEM, VMEM, ANY, ANY, VMEM, VMEM, VMEM],
        out_specs=(VMEM, VMEM, VMEM),
        scratch_shapes=[
            pltpu.VMEM((width // 2, width), jnp.bfloat16),
            pltpu.VMEM((width, width), jnp.bfloat16),
            pltpu.SemaphoreType.DMA((2,)),
        ],
        compiler_params=PARAMS,
        name="precondition",
    )(lane.reshape(1), pieces, left_root, right_root, beside, across, opposite)
    product = exchange(product.reshape(members, near * tile, quarter), ("dp", "own"), flat_groups)

    scaled = pl.pallas_call(
        graft,
        out_shape=jax.ShapeDtypeStruct((PLANES, SEATS, tile, quarter), jnp.bfloat16),
        in_specs=[VMEM],
        out_specs=VMEM,
        compiler_params=PARAMS,
        name="graft",
    )(product.reshape(members, near, tile, quarter))
    grads, grams, scaled = lax.optimization_barrier((grads, grams, scaled))
    returned = exchange(scaled.reshape(PLANES, SEATS * tile, quarter), "own", plane_groups)

    used = jnp.sum((owner_list == lax.axis_index("own")).astype(jnp.int32))
    new_left, new_right = pl.pallas_call(
        statistics,
        out_shape=(
            jax.ShapeDtypeStruct(left_stat.shape, jnp.float32),
            jax.ShapeDtypeStruct(right_stat.shape, jnp.float32),
        ),
        in_specs=[SMEM, VMEM, VMEM, HBM, HBM],
        out_specs=(HBM, HBM),
        scratch_shapes=[
            pltpu.VMEM((2, 2, quarter, width), jnp.float32),
            pltpu.VMEM((2, 2, quarter, width), jnp.float32),
            pltpu.SemaphoreType.DMA((2, 2, 2)),
        ],
        compiler_params=PARAMS,
        cost_estimate=pl.CostEstimate(flops=1, bytes_accessed=1, transcendentals=0),
        name="statistics",
    )(jnp.stack([lane, used]), grads, lane_swap(grams, 1), left_stat, right_stat)

    update = pl.pallas_call(
        take_cells,
        out_shape=jax.ShapeDtypeStruct((blocks, rows, quarter), jnp.bfloat16),
        in_specs=[SMEM, VMEM],
        out_specs=VMEM,
        compiler_params=PARAMS,
        name="take_cells",
    )(place, returned.reshape(owners * capacity, rows, quarter))
    return (new_left, new_right, update)


def solution(mesh):
    in_specs = (
        P("dp", None, "own", None),
        P(),
        P("own", "dp", None),
        P("own", "dp", None),
        P("own", "dp", None),
        P("own", "dp", None),
    )
    out_specs = (P("own", "dp", None), P("own", "dp", None), P(None, "own", "dp"))
    return jax.shard_map(body, mesh=mesh, in_specs=in_specs, out_specs=out_specs, check_vma=False)
```

```python
import jax
import jax.numpy as jnp
from jax import lax
from jax.experimental import pallas as pl
from jax.experimental.pallas import tpu as pltpu
from jax.sharding import PartitionSpec as P

decay_rate = 0.95
epsilon = 1e-06

VMEM = pl.BlockSpec(memory_space=pltpu.VMEM)
SMEM = pl.BlockSpec(memory_space=pltpu.SMEM)
ANY = pl.BlockSpec(memory_space=pl.ANY)
HBM = pl.BlockSpec(memory_space=pltpu.HBM)
PARAMS = pltpu.CompilerParams(vmem_limit_bytes=40 * 1024 * 1024)

PLANES, COLUMNS, CORES, LANES = 16, 4, 2, 4
LANE_ORDER = (2, 3, 0, 1)
COLUMN_ORDER = (2, 3, 0, 1)
FIRST_PLANE = 10
PLANE_ORDER = tuple((FIRST_PLANE + i) % PLANES for i in range(PLANES))
SEATS = COLUMNS * CORES
SEAT_ORDER = tuple(y * CORES + c for y in COLUMN_ORDER for c in range(CORES))


def split_columns(x_hbm, out_hbm, x, out, in_sems, out_sems):
    quarter = out.shape[3]
    parts = in_sems.shape[0]
    size = x.shape[0] // parts
    arriving, leaving = [], []
    for part in range(parts):
        blocks = pl.ds(part * size, size)
        arriving.append(pltpu.make_async_copy(x_hbm.at[blocks], x.at[blocks], in_sems.at[part]))
        leaving.append(
            pltpu.make_async_copy(out.at[:, blocks], out_hbm.at[:, blocks], out_sems.at[part])
        )
        arriving[part].start()
    for part in range(parts):
        arriving[part].wait()
        blocks = pl.ds(part * size, size)
        for place, lane in enumerate(LANE_ORDER):
            out[place, blocks] = x[blocks, :, lane * quarter : (lane + 1) * quarter]
        leaving[part].start()
    for copy in leaving:
        copy.wait()


def sum_and_place(place_ref, terms_ref, out_ref):
    out_ref[...] = jnp.zeros_like(out_ref)

    def step(block, carry):
        total = terms_ref[0, block].astype(jnp.float32)
        for term in range(1, terms_ref.shape[0]):
            total += terms_ref[term, block].astype(jnp.float32)
        out_ref[place_ref[block]] = total.astype(out_ref.dtype)
        return carry

    lax.fori_loop(0, terms_ref.shape[1], step, 0, unroll=8)


def take_cells(place_ref, cells_ref, out_ref):
    def step(block, carry):
        out_ref[block] = cells_ref[place_ref[block]]
        return carry

    lax.fori_loop(0, out_ref.shape[0], step, 0, unroll=8)


def fan_out(x_ref, out_hbm, slots, sems):
    for slot in range(2):
        for i, seat in enumerate(SEAT_ORDER):
            for k, plane in enumerate(PLANE_ORDER):
                slots[slot, i, plane] = x_ref[k, seat, slot]
    copies = [
        pltpu.make_async_copy(slots.at[lane % 2], out_hbm.at[i], sems.at[i])
        for i, lane in enumerate(LANE_ORDER)
    ]
    for copy in copies:
        copy.start()
    for copy in copies:
        copy.wait()


def paired(first, second):
    upper = lax.broadcasted_iota(jnp.int32, first.shape, first.ndim - 2) < 4
    return (
        jnp.where(upper, first, pltpu.roll(second, 4, first.ndim - 2)),
        jnp.where(upper, pltpu.roll(first, 4, first.ndim - 2), second),
    )


def gram_rows(block, side, near):
    rows = block[near, :] if side == 0 else block[:, near]
    dims = ((1 - side,), (1 - side,))
    return lax.dot_general(rows, block[...], (dims, ((), ())), preferred_element_type=jnp.float32)


def pick_blocks(lane_ref, left_ref, right_ref, beside_ref, across_ref, opposite_ref):
    lane = lane_ref[0]
    parity = lax.rem(lane, 2)
    quarter = left_ref.shape[1]

    def block(ref, slot, lane_of_columns):
        columns = pl.ds(pl.multiple_of(lane_of_columns * quarter, quarter), quarter)
        return ref[slot, :, columns]

    for side, ref in enumerate((left_ref, right_ref)):
        for i, column in enumerate((lane, lane ^ 3, lane ^ 2)):
            beside_ref[3 * side + i] = block(ref, 1 - parity, column)
        for i, column in enumerate((lane, lane ^ 1)):
            across_ref[2 * side + i] = block(ref, 1 - parity, column)
        opposite_ref[side] = block(ref, parity, lane)


def precondition(
    lane_ref, pieces, left_hbm, right_hbm, beside, across, opposite, grads_ref, out_ref, grams_ref,
    lefts, rights, own, sems,
):
    lane = lane_ref[0]
    parity = lax.rem(lane, 2)
    width = grads_ref.shape[0]
    quarter = left_hbm.shape[1]

    def rows_of(x):
        return pl.ds(pl.multiple_of(x * quarter, quarter), quarter)

    copies = [
        pltpu.make_async_copy(left_hbm.at[parity], own.at[0], sems.at[0]),
        pltpu.make_async_copy(right_hbm.at[parity], own.at[1], sems.at[1]),
    ]
    for copy in copies:
        copy.start()

    square = jnp.zeros((1, 1), jnp.float32)
    for i, source in enumerate(LANE_ORDER):
        even, odd = [None] * COLUMNS, [None] * COLUMNS
        for j, y in enumerate(COLUMN_ORDER):
            even[y], odd[y] = paired(
                pieces[i, j * CORES].astype(jnp.float32),
                pieces[i, j * CORES + 1].astype(jnp.float32),
            )
        value = jnp.stack([jnp.stack(even, axis=1), jnp.stack(odd, axis=1)], axis=1)
        value = value.reshape(width // 8, 8, quarter)
        sums = jnp.sum(value * value, axis=0)
        square += jnp.sum(sums, axis=(0, 1), keepdims=True)
        flat = value.reshape(width, quarter).astype(jnp.bfloat16)
        grads_ref[:, source * quarter : (source + 1) * quarter] = flat
    for copy in copies:
        copy.wait()
    beyond, far, last = lane ^ 1, lane ^ 3, lane ^ 2
    turn = lane & 2

    for side, (target, mask) in enumerate(((lefts, 0), (rights, turn))):

        def put(row, column, block):
            target[rows_of(row), rows_of(column ^ mask)] = block
            if row is not column:
                target[rows_of(column), rows_of(row ^ mask)] = block.T

        put(lane, lane, own[side, :, rows_of(lane)])
        for other in (beyond, far, last):
            put(lane, other, own[side, :, rows_of(other)])
        put(beyond, beyond, beside[3 * side])
        put(beyond, last, beside[3 * side + 1])
        put(beyond, far, beside[3 * side + 2])
        put(far, far, across[2 * side])
        put(far, last, across[2 * side + 1])
        put(last, last, opposite[side])
    half = jnp.dot(lefts[...], grads_ref[...], preferred_element_type=jnp.float32)
    product = jnp.dot(
        half.astype(jnp.bfloat16), rights[...], preferred_element_type=jnp.float32
    )
    prod_sq = jnp.sum(jnp.sum(product * product, axis=0, keepdims=True), axis=1, keepdims=True)
    cells = float(width * width)
    ratio = jnp.sqrt(square / cells) / jnp.sqrt(prod_sq / cells + epsilon)
    pairs = out_ref.shape[1]
    for i in range(2):
        block = product[:, i * quarter : (i + 1) * quarter] * ratio
        block = block.reshape(pairs, 2, COLUMNS, 8, quarter)
        for j, y in enumerate(COLUMN_ORDER):
            for core, value in enumerate(paired(block[:, 0, y], block[:, 1, y])):
                out_ref[i * SEATS + j * CORES + core] = value.astype(out_ref.dtype)
    for side in range(2):
        grams_ref[side] = gram_rows(grads_ref, side, rows_of(lane ^ 1)).astype(grams_ref.dtype)


def regroup(x_ref, out_ref):
    for j, seat in enumerate(SEAT_ORDER):
        tiles = [x_ref[slot * SEATS + j].astype(jnp.float32) for slot in range(2)]
        for odd, value in enumerate(paired(*tiles)):
            for p in range(value.shape[0]):
                place = (2 * p + odd - FIRST_PLANE) % PLANES
                out_ref[place, seat] = value[p].astype(out_ref.dtype)


def statistics(
    info_ref, block, grams_ref, left_hbm, right_hbm, new_left_hbm, new_right_hbm, old, new, sems
):
    lane, used = info_ref[0], info_ref[1]
    parity = lax.rem(lane, 2)
    slots = (parity, 1 - parity)
    width = block.shape[0]
    quarter = old.shape[2]
    loads, stores = [], []
    for i, slot in enumerate(slots):
        for side, (src, target) in enumerate(((left_hbm, new_left_hbm), (right_hbm, new_right_hbm))):
            loads.append(pltpu.make_async_copy(src.at[slot], old.at[i, side], sems.at[0, i, side]))
            stores.append(pltpu.make_async_copy(new.at[i, side], target.at[slot], sems.at[1, i, side]))
    for copy in loads:
        copy.start()
    mine = pl.ds(pl.multiple_of(lane * quarter, quarter), quarter)
    for i, slot in enumerate(slots):
        for side in range(2):
            if i == 0:
                gram = gram_rows(block, side, mine)
            else:
                gram = grams_ref[side].astype(jnp.float32)
            loads[2 * i + side].wait()
            was = old[i, side]
            new[i, side] = jnp.where(slot < used, decay_rate * was + gram / width, was)
            stores[2 * i + side].start()
    for copy in stores:
        copy.wait()


def lane_swap(x, mask):
    return lax.ppermute(x, "dp", [(i, i ^ mask) for i in range(LANES)])


def exchange(x, axes, groups):
    return lax.all_to_all(
        x, axes, split_axis=0, concat_axis=0, tiled=True, axis_index_groups=groups
    )


def body(partial_grads, owner_list, left_stat, right_stat, left_root, right_root):
    owners = PLANES * SEATS
    capacity, quarter, width = left_stat.shape
    blocks = owner_list.shape[0]
    rows = width // owners
    block_ids = jnp.arange(blocks, dtype=jnp.int32)
    lane = lax.axis_index("dp")
    lane_groups = [list(LANE_ORDER)]
    plane_groups = [[z * SEATS + seat for z in PLANE_ORDER] for seat in range(SEATS)]
    flat_groups = [
        [x * owners + z * SEATS + seat for x in LANE_ORDER for seat in SEAT_ORDER]
        for z in range(PLANES)
    ]

    half_groups = [
        [x * owners + z * SEATS + seat for x in (half, half + 1) for seat in SEAT_ORDER]
        for half in (0, 2)
        for z in range(PLANES)
    ]

    terms = pl.pallas_call(
        split_columns,
        out_shape=jax.ShapeDtypeStruct((LANES, blocks, rows, quarter), jnp.bfloat16),
        in_specs=[HBM],
        out_specs=HBM,
        scratch_shapes=[
            pltpu.VMEM((blocks, rows, width), jnp.bfloat16),
            pltpu.VMEM((LANES, blocks, rows, quarter), jnp.bfloat16),
            pltpu.SemaphoreType.DMA((4,)),
            pltpu.SemaphoreType.DMA((4,)),
        ],
        name="split_columns",
    )(partial_grads[0])
    left, right, terms = lax.optimization_barrier((left_root, right_root, terms))
    terms = exchange(terms, "dp", lane_groups)
    picked = pl.pallas_call(
        pick_blocks,
        out_shape=[jax.ShapeDtypeStruct((n, quarter, quarter), jnp.bfloat16) for n in (6, 4, 2)],
        in_specs=[SMEM, VMEM, VMEM],
        out_specs=[VMEM] * 3,
        compiler_params=PARAMS,
        cost_estimate=pl.CostEstimate(flops=1, bytes_accessed=4 * 1024 * 1024, transcendentals=0),
        name="pick_blocks",
    )(lane.reshape(1), left, right)

    opposite = lane_swap(picked[2], 2)

    same = (owner_list[:, None] == owner_list[None, :]) & (block_ids[None, :] < block_ids[:, None])
    slot_index = jnp.sum(same.astype(jnp.int32), axis=1)
    turned = lax.rem(owner_list + (PLANES - FIRST_PLANE) * SEATS, owners)
    place = turned * capacity + slot_index

    outgoing = pl.pallas_call(
        sum_and_place,
        out_shape=jax.ShapeDtypeStruct((owners * capacity, rows, quarter), jnp.bfloat16),
        in_specs=[SMEM, VMEM],
        out_specs=VMEM,
        compiler_params=PARAMS,
        name="sum_and_place",
    )(place, terms)
    outgoing = outgoing.reshape(PLANES, SEATS * capacity * rows, quarter)
    picked, opposite, outgoing = lax.optimization_barrier((picked, opposite, outgoing))
    arrived = exchange(outgoing, "own", plane_groups)
    beside, across = lane_swap(picked[0], 1), lane_swap(picked[1], 3)
    beside, across, arrived = lax.optimization_barrier((beside, across, arrived))

    tile = capacity * rows
    copies = pl.pallas_call(
        fan_out,
        out_shape=jax.ShapeDtypeStruct((LANES, SEATS, PLANES, rows, quarter), jnp.bfloat16),
        in_specs=[VMEM],
        out_specs=HBM,
        scratch_shapes=[
            pltpu.VMEM((capacity, SEATS, PLANES, rows, quarter), jnp.bfloat16),
            pltpu.SemaphoreType.DMA((LANES,)),
        ],
        compiler_params=PARAMS,
        name="fan_out",
    )(arrived.reshape(PLANES, SEATS, capacity, rows, quarter))
    members = LANES * SEATS
    pieces = exchange(copies.reshape(members, PLANES * rows, quarter), ("dp", "own"), flat_groups)
    pieces = pieces.reshape(LANES, SEATS, PLANES // 2, 2 * rows, quarter)

    grads, product, grams = pl.pallas_call(
        precondition,
        out_shape=(
            jax.ShapeDtypeStruct((width, width), jnp.bfloat16),
            jax.ShapeDtypeStruct((members // 2, PLANES // 2, tile, quarter), jnp.bfloat16),
            jax.ShapeDtypeStruct((2, quarter, width), jnp.bfloat16),
        ),
        in_specs=[SMEM, VMEM, ANY, ANY, VMEM, VMEM, VMEM],
        out_specs=(VMEM, VMEM, VMEM),
        scratch_shapes=[
            pltpu.VMEM((width, width), jnp.bfloat16),
            pltpu.VMEM((width, width), jnp.bfloat16),
            pltpu.VMEM((2, quarter, width), jnp.bfloat16),
            pltpu.SemaphoreType.DMA((2,)),
        ],
        compiler_params=PARAMS,
        name="precondition",
    )(lane.reshape(1), pieces, left_root, right_root, beside, across, opposite)
    product = exchange(
        product.reshape(members // 2, PLANES // 2 * tile, quarter), ("dp", "own"), half_groups
    )

    scaled = pl.pallas_call(
        regroup,
        out_shape=jax.ShapeDtypeStruct((PLANES, SEATS, tile, quarter), jnp.bfloat16),
        in_specs=[VMEM],
        out_specs=VMEM,
        compiler_params=PARAMS,
        name="regroup",
    )(product.reshape(members // 2, PLANES // 2, tile, quarter))
    grads, grams, scaled = lax.optimization_barrier((grads, grams, scaled))
    returned = exchange(scaled.reshape(PLANES, SEATS * tile, quarter), "own", plane_groups)

    used = jnp.sum((owner_list == lax.axis_index("own")).astype(jnp.int32))
    new_left, new_right = pl.pallas_call(
        statistics,
        out_shape=(
            jax.ShapeDtypeStruct(left_stat.shape, jnp.float32),
            jax.ShapeDtypeStruct(right_stat.shape, jnp.float32),
        ),
        in_specs=[SMEM, VMEM, VMEM, HBM, HBM],
        out_specs=(HBM, HBM),
        scratch_shapes=[
            pltpu.VMEM((2, 2, quarter, width), jnp.float32),
            pltpu.VMEM((2, 2, quarter, width), jnp.float32),
            pltpu.SemaphoreType.DMA((2, 2, 2)),
        ],
        compiler_params=PARAMS,
        cost_estimate=pl.CostEstimate(flops=1, bytes_accessed=1, transcendentals=0),
        name="statistics",
    )(jnp.stack([lane, used]), grads, lane_swap(grams, 1), left_stat, right_stat)

    update = pl.pallas_call(
        take_cells,
        out_shape=jax.ShapeDtypeStruct((blocks, rows, quarter), jnp.bfloat16),
        in_specs=[SMEM, VMEM],
        out_specs=VMEM,
        compiler_params=PARAMS,
        name="take_cells",
    )(place, returned.reshape(owners * capacity, rows, quarter))
    return (new_left, new_right, update)


def solution(mesh):
    in_specs = (
        P("dp", None, "own", None),
        P(),
        P("own", "dp", None),
        P("own", "dp", None),
        P("own", "dp", None),
        P("own", "dp", None),
    )
    out_specs = (P("own", "dp", None), P("own", "dp", None), P(None, "own", "dp"))
    return jax.shard_map(body, mesh=mesh, in_specs=in_specs, out_specs=out_specs, check_vma=False)
```

```python
import jax
import jax.numpy as jnp
from jax import lax
from jax.experimental import pallas as pl
from jax.experimental.pallas import tpu as pltpu
from jax.sharding import PartitionSpec as P

decay_rate = 0.95
epsilon = 1e-06

VMEM = pl.BlockSpec(memory_space=pltpu.VMEM)
SMEM = pl.BlockSpec(memory_space=pltpu.SMEM)
HBM = pl.BlockSpec(memory_space=pltpu.HBM)
PARAMS = pltpu.CompilerParams(vmem_limit_bytes=40 * 1024 * 1024)

PLANES, COLUMNS, CORES, LANES = 16, 4, 2, 4
LANE_ORDER = (2, 3, 0, 1)
COLUMN_ORDER = (2, 3, 0, 1)
FIRST_PLANE = 10
PLANE_ORDER = tuple((FIRST_PLANE + i) % PLANES for i in range(PLANES))
SEATS = COLUMNS * CORES
SEAT_ORDER = tuple(y * CORES + c for y in COLUMN_ORDER for c in range(CORES))


def split_columns(x_hbm, out_hbm, x, out, in_sems, out_sems):
    quarter = out.shape[3]
    parts = in_sems.shape[0]
    size = x.shape[0] // parts
    arriving, leaving = [], []
    for part in range(parts):
        blocks = pl.ds(part * size, size)
        arriving.append(pltpu.make_async_copy(x_hbm.at[blocks], x.at[blocks], in_sems.at[part]))
        leaving.append(
            pltpu.make_async_copy(out.at[:, blocks], out_hbm.at[:, blocks], out_sems.at[part])
        )
        arriving[part].start()
    for part in range(parts):
        arriving[part].wait()
        blocks = pl.ds(part * size, size)
        for place, lane in enumerate(LANE_ORDER):
            out[place, blocks] = x[blocks, :, lane * quarter : (lane + 1) * quarter]
        leaving[part].start()
    for copy in leaving:
        copy.wait()


def sum_and_place(cell_ref, terms_ref, out_ref):
    out_ref[...] = jnp.zeros_like(out_ref)

    def step(pair, carry):
        total = terms_ref[0, pair].astype(jnp.float32)
        for term in range(1, terms_ref.shape[0]):
            total += terms_ref[term, pair].astype(jnp.float32)
        out_ref[cell_ref[2 * pair]] = total[:4].astype(out_ref.dtype)
        out_ref[cell_ref[2 * pair + 1]] = total[4:].astype(out_ref.dtype)
        return carry

    lax.fori_loop(0, terms_ref.shape[1], step, 0, unroll=32)


def take_cells(place_ref, cells_ref, out_ref):
    def step(block, carry):
        out_ref[block] = cells_ref[place_ref[block]]
        return carry

    lax.fori_loop(0, out_ref.shape[0], step, 0, unroll=32)


def fan_out(x_ref, out_ref):
    for i, seat in enumerate(SEAT_ORDER):
        for k, plane in enumerate(PLANE_ORDER):
            for slot in range(2):
                value = x_ref[k, seat, slot]
                for place, lane in enumerate(LANE_ORDER):
                    if lane % 2 == slot:
                        out_ref[place, i, plane] = value


def paired(first, second):
    upper = lax.broadcasted_iota(jnp.int32, first.shape, first.ndim - 2) < 4
    return (
        jnp.where(upper, first, pltpu.roll(second, 4, first.ndim - 2)),
        jnp.where(upper, pltpu.roll(first, 4, first.ndim - 2), second),
    )


def gram_rows(block, side, near):
    rows = block[near, :] if side == 0 else block[:, near]
    dims = ((1 - side,), (1 - side,))
    return lax.dot_general(rows, block[...], (dims, ((), ())), preferred_element_type=jnp.float32)


def pick_blocks(lane_ref, left_ref, right_ref, beside_ref, across_ref, opposite_ref):
    lane = lane_ref[0]
    parity = lax.rem(lane, 2)
    quarter = left_ref.shape[1]

    def block(ref, slot, lane_of_columns):
        columns = pl.ds(pl.multiple_of(lane_of_columns * quarter, quarter), quarter)
        return ref[slot, :, columns]

    for side, ref in enumerate((left_ref, right_ref)):
        for i, column in enumerate((lane, lane ^ 3, lane ^ 2)):
            beside_ref[3 * side + i] = block(ref, 1 - parity, column)
        for i, column in enumerate((lane, lane ^ 1)):
            across_ref[2 * side + i] = block(ref, 1 - parity, column)
        opposite_ref[side] = block(ref, parity, lane)


def assemble(lane_ref, own_left_ref, own_right_ref, beside, across, opposite, lefts, rights):
    lane = lane_ref[0]
    parity = lax.rem(lane, 2)
    quarter = own_left_ref.shape[1]

    def rows_of(x):
        return pl.ds(pl.multiple_of(x * quarter, quarter), quarter)

    beyond, far, last = lane ^ 1, lane ^ 3, lane ^ 2
    turn = lane & 2

    for side, (own, target, mask) in enumerate(
        ((own_left_ref, lefts, 0), (own_right_ref, rights, turn))
    ):

        def put(row, column, block):
            target[rows_of(row), rows_of(column ^ mask)] = block
            if row is not column:
                target[rows_of(column), rows_of(row ^ mask)] = block.T

        put(lane, lane, own[parity, :, rows_of(lane)])
        for other in (beyond, far, last):
            put(lane, other, own[parity, :, rows_of(other)])
        put(beyond, beyond, beside[3 * side])
        put(beyond, last, beside[3 * side + 1])
        put(beyond, far, beside[3 * side + 2])
        put(far, far, across[2 * side])
        put(far, last, across[2 * side + 1])
        put(last, last, opposite[side])


def precondition(lane_ref, pieces, left_ref, right_ref, grads_ref, out_ref, grams_ref):
    lane = lane_ref[0]
    width = grads_ref.shape[0]
    quarter = width // LANES

    def rows_of(x):
        return pl.ds(pl.multiple_of(x * quarter, quarter), quarter)

    square = jnp.zeros((1, 1), jnp.float32)
    for i, source in enumerate(LANE_ORDER):
        even, odd = [None] * COLUMNS, [None] * COLUMNS
        for j, y in enumerate(COLUMN_ORDER):
            even[y], odd[y] = paired(
                pieces[i, j * CORES].astype(jnp.float32),
                pieces[i, j * CORES + 1].astype(jnp.float32),
            )
        value = jnp.stack([jnp.stack(even, axis=1), jnp.stack(odd, axis=1)], axis=1)
        value = value.reshape(width // 8, 8, quarter)
        sums = jnp.sum(value * value, axis=0)
        square += jnp.sum(sums, axis=(0, 1), keepdims=True)
        flat = value.reshape(width, quarter).astype(jnp.bfloat16)
        grads_ref[:, source * quarter : (source + 1) * quarter] = flat
    half = jnp.dot(left_ref[...], grads_ref[...], preferred_element_type=jnp.float32)
    product = jnp.dot(
        half.astype(jnp.bfloat16), right_ref[...], preferred_element_type=jnp.float32
    )
    prod_sq = jnp.sum(jnp.sum(product * product, axis=0, keepdims=True), axis=1, keepdims=True)
    cells = float(width * width)
    ratio = jnp.sqrt(square / cells) / jnp.sqrt(prod_sq / cells + epsilon)
    pairs = out_ref.shape[1]
    for i in range(2):
        block = product[:, i * quarter : (i + 1) * quarter] * ratio
        block = block.reshape(pairs, 2, COLUMNS, 8, quarter)
        for j, y in enumerate(COLUMN_ORDER):
            for core, value in enumerate(paired(block[:, 0, y], block[:, 1, y])):
                out_ref[i * SEATS + j * CORES + core] = value.astype(out_ref.dtype)
    for side in range(2):
        grams_ref[side] = gram_rows(grads_ref, side, rows_of(lane ^ 1)).astype(grams_ref.dtype)


def regroup(x_ref, out_ref):
    for j, seat in enumerate(SEAT_ORDER):
        tiles = [x_ref[slot * SEATS + j].astype(jnp.float32) for slot in range(2)]
        for odd, value in enumerate(paired(*tiles)):
            for p in range(value.shape[0]):
                place = (2 * p + odd - FIRST_PLANE) % PLANES
                out_ref[place, seat] = value[p].astype(out_ref.dtype)


def statistics(
    info_ref, block, grams_ref, left_hbm, right_hbm, new_left_hbm, new_right_hbm, old, new, sems
):
    lane, used = info_ref[0], info_ref[1]
    parity = lax.rem(lane, 2)
    slots = (parity, 1 - parity)
    width = block.shape[0]
    quarter = old.shape[2]
    loads, stores = [], []
    for i, slot in enumerate(slots):
        for side, (src, target) in enumerate(((left_hbm, new_left_hbm), (right_hbm, new_right_hbm))):
            loads.append(pltpu.make_async_copy(src.at[slot], old.at[i, side], sems.at[0, i, side]))
            stores.append(pltpu.make_async_copy(new.at[i, side], target.at[slot], sems.at[1, i, side]))
    for copy in loads:
        copy.start()
    mine = pl.ds(pl.multiple_of(lane * quarter, quarter), quarter)
    for i, slot in enumerate(slots):
        for side in range(2):
            if i == 0:
                gram = gram_rows(block, side, mine)
            else:
                gram = grams_ref[side].astype(jnp.float32)
            loads[2 * i + side].wait()
            was = old[i, side]
            new[i, side] = jnp.where(slot < used, decay_rate * was + gram / width, was)
            stores[2 * i + side].start()
    for copy in stores:
        copy.wait()


def lane_swap(x, mask):
    return lax.ppermute(x, "dp", [(i, i ^ mask) for i in range(LANES)])


def exchange(x, axes, groups):
    return lax.all_to_all(
        x, axes, split_axis=0, concat_axis=0, tiled=True, axis_index_groups=groups
    )


def body(partial_grads, owner_list, left_stat, right_stat, left_root, right_root):
    owners = PLANES * SEATS
    capacity, quarter, width = left_stat.shape
    blocks = owner_list.shape[0]
    rows = width // owners
    block_ids = jnp.arange(blocks, dtype=jnp.int32)
    lane = lax.axis_index("dp")
    lane_groups = [list(LANE_ORDER)]
    plane_groups = [[z * SEATS + seat for z in PLANE_ORDER] for seat in range(SEATS)]
    flat_groups = [
        [x * owners + z * SEATS + seat for x in LANE_ORDER for seat in SEAT_ORDER]
        for z in range(PLANES)
    ]

    half_groups = [
        [x * owners + z * SEATS + seat for x in (half, half + 1) for seat in SEAT_ORDER]
        for half in (0, 2)
        for z in range(PLANES)
    ]

    terms = pl.pallas_call(
        split_columns,
        out_shape=jax.ShapeDtypeStruct((LANES, blocks, rows, quarter), jnp.bfloat16),
        in_specs=[HBM],
        out_specs=HBM,
        scratch_shapes=[
            pltpu.VMEM((blocks, rows, width), jnp.bfloat16),
            pltpu.VMEM((LANES, blocks, rows, quarter), jnp.bfloat16),
            pltpu.SemaphoreType.DMA((4,)),
            pltpu.SemaphoreType.DMA((4,)),
        ],
        name="split_columns",
    )(partial_grads[0])
    left, right, terms = lax.optimization_barrier((left_root, right_root, terms))
    terms = exchange(terms, "dp", lane_groups)
    picked = pl.pallas_call(
        pick_blocks,
        out_shape=[jax.ShapeDtypeStruct((n, quarter, quarter), jnp.bfloat16) for n in (6, 4, 2)],
        in_specs=[SMEM, VMEM, VMEM],
        out_specs=[VMEM] * 3,
        compiler_params=PARAMS,
        cost_estimate=pl.CostEstimate(flops=1, bytes_accessed=4 * 1024 * 1024, transcendentals=0),
        name="pick_blocks",
    )(lane.reshape(1), left, right)

    opposite = lane_swap(picked[2], 2)

    same = (owner_list[:, None] == owner_list[None, :]) & (block_ids[None, :] < block_ids[:, None])
    slot_index = jnp.sum(same.astype(jnp.int32), axis=1)
    turned = lax.rem(owner_list + (PLANES - FIRST_PLANE) * SEATS, owners)
    place = turned * capacity + slot_index

    outgoing = pl.pallas_call(
        sum_and_place,
        out_shape=jax.ShapeDtypeStruct((owners * capacity, rows, quarter), jnp.bfloat16),
        in_specs=[SMEM, VMEM],
        out_specs=VMEM,
        compiler_params=PARAMS,
        name="sum_and_place",
    )(place, terms.reshape(LANES, blocks // 2, 2 * rows, quarter))
    outgoing = outgoing.reshape(PLANES, SEATS * capacity * rows, quarter)
    picked, opposite, outgoing = lax.optimization_barrier((picked, opposite, outgoing))
    arrived = exchange(outgoing, "own", plane_groups)
    beside, across = lane_swap(picked[0], 1), lane_swap(picked[1], 3)
    lefts, rights = pl.pallas_call(
        assemble,
        out_shape=[jax.ShapeDtypeStruct((width, width), jnp.bfloat16)] * 2,
        in_specs=[SMEM] + [VMEM] * 5,
        out_specs=[VMEM] * 2,
        compiler_params=PARAMS,
        name="assemble",
    )(lane.reshape(1), left, right, beside, across, opposite)
    lefts, rights, arrived = lax.optimization_barrier((lefts, rights, arrived))

    tile = capacity * rows
    copies = pl.pallas_call(
        fan_out,
        out_shape=jax.ShapeDtypeStruct((LANES, SEATS, PLANES, rows, quarter), jnp.bfloat16),
        in_specs=[VMEM],
        out_specs=VMEM,
        compiler_params=PARAMS,
        name="fan_out",
    )(arrived.reshape(PLANES, SEATS, capacity, rows, quarter))
    members = LANES * SEATS
    pieces = exchange(copies.reshape(members, PLANES * rows, quarter), ("dp", "own"), flat_groups)
    pieces = pieces.reshape(LANES, SEATS, PLANES // 2, 2 * rows, quarter)

    grads, product, grams = pl.pallas_call(
        precondition,
        out_shape=(
            jax.ShapeDtypeStruct((width, width), jnp.bfloat16),
            jax.ShapeDtypeStruct((members // 2, PLANES // 2, tile, quarter), jnp.bfloat16),
            jax.ShapeDtypeStruct((2, quarter, width), jnp.bfloat16),
        ),
        in_specs=[SMEM, VMEM, VMEM, VMEM],
        out_specs=(VMEM, VMEM, VMEM),
        compiler_params=PARAMS,
        name="precondition",
    )(lane.reshape(1), pieces, lefts, rights)
    product = exchange(
        product.reshape(members // 2, PLANES // 2 * tile, quarter), ("dp", "own"), half_groups
    )

    scaled = pl.pallas_call(
        regroup,
        out_shape=jax.ShapeDtypeStruct((PLANES, SEATS, tile, quarter), jnp.bfloat16),
        in_specs=[VMEM],
        out_specs=VMEM,
        compiler_params=PARAMS,
        name="regroup",
    )(product.reshape(members // 2, PLANES // 2, tile, quarter))
    grads, grams, scaled = lax.optimization_barrier((grads, grams, scaled))
    returned = exchange(scaled.reshape(PLANES, SEATS * tile, quarter), "own", plane_groups)

    used = jnp.sum((owner_list == lax.axis_index("own")).astype(jnp.int32))
    new_left, new_right = pl.pallas_call(
        statistics,
        out_shape=(
            jax.ShapeDtypeStruct(left_stat.shape, jnp.float32),
            jax.ShapeDtypeStruct(right_stat.shape, jnp.float32),
        ),
        in_specs=[SMEM, VMEM, VMEM, HBM, HBM],
        out_specs=(HBM, HBM),
        scratch_shapes=[
            pltpu.VMEM((2, 2, quarter, width), jnp.float32),
            pltpu.VMEM((2, 2, quarter, width), jnp.float32),
            pltpu.SemaphoreType.DMA((2, 2, 2)),
        ],
        compiler_params=PARAMS,
        cost_estimate=pl.CostEstimate(flops=1, bytes_accessed=1, transcendentals=0),
        name="statistics",
    )(jnp.stack([lane, used]), grads, lane_swap(grams, 1), left_stat, right_stat)

    update = pl.pallas_call(
        take_cells,
        out_shape=jax.ShapeDtypeStruct((blocks, rows, quarter), jnp.bfloat16),
        in_specs=[SMEM, VMEM],
        out_specs=VMEM,
        compiler_params=PARAMS,
        name="take_cells",
    )(place, returned.reshape(owners * capacity, rows, quarter))
    return (new_left, new_right, update)


def solution(mesh):
    in_specs = (
        P("dp", None, "own", None),
        P(),
        P("own", "dp", None),
        P("own", "dp", None),
        P("own", "dp", None),
        P("own", "dp", None),
    )
    out_specs = (P("own", "dp", None), P("own", "dp", None), P(None, "own", "dp"))
    return jax.shard_map(body, mesh=mesh, in_specs=in_specs, out_specs=out_specs, check_vma=False)
```

```python
import jax
import jax.numpy as jnp
from jax import lax
from jax.experimental import pallas as pl
from jax.experimental.pallas import tpu as pltpu
from jax.sharding import PartitionSpec as P

decay_rate = 0.95
epsilon = 1e-06

VMEM = pl.BlockSpec(memory_space=pltpu.VMEM)
SMEM = pl.BlockSpec(memory_space=pltpu.SMEM)
HBM = pl.BlockSpec(memory_space=pltpu.HBM)
PARAMS = pltpu.CompilerParams(vmem_limit_bytes=40 * 1024 * 1024)

PLANES, COLUMNS, CORES, LANES = 16, 4, 2, 4
LANE_ORDER = (2, 3, 0, 1)
COLUMN_ORDER = (2, 3, 0, 1)
FIRST_PLANE = 11
PLANE_ORDER = tuple((FIRST_PLANE + i) % PLANES for i in range(PLANES))
SEATS = COLUMNS * CORES
SEAT_ORDER = tuple(y * CORES + c for y in COLUMN_ORDER for c in range(CORES))


def split_columns(x_hbm, out_hbm, x, out, in_sems, out_sems):
    quarter = out.shape[3]
    parts = in_sems.shape[0]
    size = x.shape[0] // parts
    arriving, leaving = [], []
    for part in range(parts):
        blocks = pl.ds(part * size, size)
        arriving.append(pltpu.make_async_copy(x_hbm.at[blocks], x.at[blocks], in_sems.at[part]))
        leaving.append(
            pltpu.make_async_copy(out.at[:, blocks], out_hbm.at[:, blocks], out_sems.at[part])
        )
        arriving[part].start()
    for part in range(parts):
        arriving[part].wait()
        blocks = pl.ds(part * size, size)
        for place, lane in enumerate(LANE_ORDER):
            out[place, blocks] = x[blocks, :, lane * quarter : (lane + 1) * quarter]
        leaving[part].start()
    for copy in leaving:
        copy.wait()


def sum_and_place(cell_ref, terms_ref, out_ref):
    out_ref[...] = jnp.zeros_like(out_ref)

    def step(pair, carry):
        total = terms_ref[0, pair].astype(jnp.float32)
        for term in range(1, terms_ref.shape[0]):
            total += terms_ref[term, pair].astype(jnp.float32)
        out_ref[cell_ref[2 * pair]] = total[:4].astype(out_ref.dtype)
        out_ref[cell_ref[2 * pair + 1]] = total[4:].astype(out_ref.dtype)
        return carry

    lax.fori_loop(0, terms_ref.shape[1], step, 0, unroll=32)


def take_cells(cell_ref, cells_ref, out_hbm, out, sems):
    parts = sems.shape[0]
    size = out.shape[0] // parts

    def step(block, carry):
        out[block] = cells_ref[cell_ref[block]]
        return carry

    copies = []
    for part in range(parts):
        blocks = pl.ds(part * size, size)
        lax.fori_loop(part * size, (part + 1) * size, step, 0, unroll=32)
        copy = pltpu.make_async_copy(out.at[blocks], out_hbm.at[blocks], sems.at[part])
        copy.start()
        copies.append(copy)
    for copy in copies:
        copy.wait()


def fan_out(x_ref, out_ref):
    for i, seat in enumerate(SEAT_ORDER):
        for k, plane in enumerate(PLANE_ORDER):
            for slot in range(2):
                value = x_ref[k, seat, slot]
                for place, lane in enumerate(LANE_ORDER):
                    if lane % 2 == slot:
                        out_ref[place, i, plane] = value


def paired(first, second):
    upper = lax.broadcasted_iota(jnp.int32, first.shape, first.ndim - 2) < 4
    return (
        jnp.where(upper, first, pltpu.roll(second, 4, first.ndim - 2)),
        jnp.where(upper, pltpu.roll(first, 4, first.ndim - 2), second),
    )


def gram_rows(block, side, near):
    rows = block[near, :] if side == 0 else block[:, near]
    dims = ((1 - side,), (1 - side,))
    return lax.dot_general(rows, block[...], (dims, ((), ())), preferred_element_type=jnp.float32)


def pick_blocks(lane_ref, left_ref, right_ref, beside_ref, across_ref, opposite_ref):
    lane = lane_ref[0]
    parity = lax.rem(lane, 2)
    quarter = left_ref.shape[1]

    def block(ref, slot, lane_of_columns):
        columns = pl.ds(pl.multiple_of(lane_of_columns * quarter, quarter), quarter)
        return ref[slot, :, columns]

    for side, ref in enumerate((left_ref, right_ref)):
        for i, column in enumerate((lane, lane ^ 3, lane ^ 2)):
            beside_ref[3 * side + i] = block(ref, 1 - parity, column)
        for i, column in enumerate((lane, lane ^ 1)):
            across_ref[2 * side + i] = block(ref, 1 - parity, column)
        opposite_ref[side] = block(ref, parity, lane)


def assemble(lane_ref, own_left_ref, own_right_ref, beside, across, opposite, lefts, rights):
    lane = lane_ref[0]
    parity = lax.rem(lane, 2)
    quarter = own_left_ref.shape[1]

    def rows_of(x):
        return pl.ds(pl.multiple_of(x * quarter, quarter), quarter)

    beyond, far, last = lane ^ 1, lane ^ 3, lane ^ 2
    turn = lane & 2

    for side, (own, target, mask) in enumerate(
        ((own_left_ref, lefts, 0), (own_right_ref, rights, turn))
    ):

        def put(row, column, block):
            target[rows_of(row), rows_of(column ^ mask)] = block
            if row is not column:
                target[rows_of(column), rows_of(row ^ mask)] = block.T

        put(lane, lane, own[parity, :, rows_of(lane)])
        for other in (beyond, far, last):
            put(lane, other, own[parity, :, rows_of(other)])
        put(beyond, beyond, beside[3 * side])
        put(beyond, last, beside[3 * side + 1])
        put(beyond, far, beside[3 * side + 2])
        put(far, far, across[2 * side])
        put(far, last, across[2 * side + 1])
        put(last, last, opposite[side])


def precondition(lane_ref, pieces, left_ref, right_ref, grads_ref, out_ref, grams_ref):
    lane = lane_ref[0]
    width = grads_ref.shape[0]
    quarter = width // LANES

    def rows_of(x):
        return pl.ds(pl.multiple_of(x * quarter, quarter), quarter)

    square = jnp.zeros((1, 1), jnp.float32)
    for i, source in enumerate(LANE_ORDER):
        even, odd = [None] * COLUMNS, [None] * COLUMNS
        for j, y in enumerate(COLUMN_ORDER):
            even[y], odd[y] = paired(
                pieces[i, j * CORES].astype(jnp.float32),
                pieces[i, j * CORES + 1].astype(jnp.float32),
            )
        value = jnp.stack([jnp.stack(even, axis=1), jnp.stack(odd, axis=1)], axis=1)
        value = value.reshape(width // 8, 8, quarter)
        sums = jnp.sum(value * value, axis=0)
        square += jnp.sum(sums, axis=(0, 1), keepdims=True)
        flat = value.reshape(width, quarter).astype(jnp.bfloat16)
        grads_ref[:, source * quarter : (source + 1) * quarter] = flat
    half = jnp.dot(left_ref[...], grads_ref[...], preferred_element_type=jnp.float32)
    product = jnp.dot(
        half.astype(jnp.bfloat16), right_ref[...], preferred_element_type=jnp.float32
    )
    prod_sq = jnp.sum(jnp.sum(product * product, axis=0, keepdims=True), axis=1, keepdims=True)
    cells = float(width * width)
    ratio = jnp.sqrt(square / cells) / jnp.sqrt(prod_sq / cells + epsilon)
    pairs = out_ref.shape[1]
    for i in range(2):
        block = product[:, i * quarter : (i + 1) * quarter] * ratio
        block = block.reshape(pairs, 2, COLUMNS, 8, quarter)
        for j, y in enumerate(COLUMN_ORDER):
            for core, value in enumerate(paired(block[:, 0, y], block[:, 1, y])):
                out_ref[i * SEATS + j * CORES + core] = value.astype(out_ref.dtype)
    for side in range(2):
        grams_ref[side] = gram_rows(grads_ref, side, rows_of(lane ^ 1)).astype(grams_ref.dtype)


def regroup(x_ref, out_ref):
    for j, seat in enumerate(SEAT_ORDER):
        tiles = [x_ref[slot * SEATS + j].astype(jnp.float32) for slot in range(2)]
        for odd, value in enumerate(paired(*tiles)):
            for p in range(value.shape[0]):
                place = (2 * p + odd - FIRST_PLANE) % PLANES
                out_ref[place, seat] = value[p].astype(out_ref.dtype)


def statistics(
    info_ref, block, grams_ref, left_hbm, right_hbm, new_left_hbm, new_right_hbm, old, new, sems
):
    lane, used = info_ref[0], info_ref[1]
    parity = lax.rem(lane, 2)
    slots = (parity, 1 - parity)
    width = block.shape[0]
    quarter = old.shape[2]
    loads, stores = [], []
    for i, slot in enumerate(slots):
        for side, (src, target) in enumerate(((left_hbm, new_left_hbm), (right_hbm, new_right_hbm))):
            loads.append(pltpu.make_async_copy(src.at[slot], old.at[i, side], sems.at[0, i, side]))
            stores.append(pltpu.make_async_copy(new.at[i, side], target.at[slot], sems.at[1, i, side]))
    for copy in loads:
        copy.start()
    mine = pl.ds(pl.multiple_of(lane * quarter, quarter), quarter)
    for i, slot in enumerate(slots):
        for side in range(2):
            if i == 0:
                gram = gram_rows(block, side, mine)
            else:
                gram = grams_ref[side].astype(jnp.float32)
            loads[2 * i + side].wait()
            was = old[i, side]
            new[i, side] = jnp.where(slot < used, decay_rate * was + gram / width, was)
            stores[2 * i + side].start()
    for copy in stores:
        copy.wait()


def lane_swap(x, mask):
    return lax.ppermute(x, "dp", [(i, i ^ mask) for i in range(LANES)])


def exchange(x, axes, groups):
    return lax.all_to_all(
        x, axes, split_axis=0, concat_axis=0, tiled=True, axis_index_groups=groups
    )


def body(partial_grads, owner_list, left_stat, right_stat, left_root, right_root):
    owners = PLANES * SEATS
    capacity, quarter, width = left_stat.shape
    blocks = owner_list.shape[0]
    rows = width // owners
    block_ids = jnp.arange(blocks, dtype=jnp.int32)
    lane = lax.axis_index("dp")
    lane_groups = [list(LANE_ORDER)]
    plane_groups = [[z * SEATS + seat for z in PLANE_ORDER] for seat in range(SEATS)]
    flat_groups = [
        [x * owners + z * SEATS + seat for x in LANE_ORDER for seat in SEAT_ORDER]
        for z in range(PLANES)
    ]

    half_groups = [
        [x * owners + z * SEATS + seat for x in (half, half + 1) for seat in SEAT_ORDER]
        for half in (0, 2)
        for z in range(PLANES)
    ]

    terms = pl.pallas_call(
        split_columns,
        out_shape=jax.ShapeDtypeStruct((LANES, blocks, rows, quarter), jnp.bfloat16),
        in_specs=[HBM],
        out_specs=HBM,
        scratch_shapes=[
            pltpu.VMEM((blocks, rows, width), jnp.bfloat16),
            pltpu.VMEM((LANES, blocks, rows, quarter), jnp.bfloat16),
            pltpu.SemaphoreType.DMA((4,)),
            pltpu.SemaphoreType.DMA((4,)),
        ],
        name="split_columns",
    )(partial_grads[0])
    left, right, terms = lax.optimization_barrier((left_root, right_root, terms))
    terms = exchange(terms, "dp", lane_groups)
    picked = pl.pallas_call(
        pick_blocks,
        out_shape=[jax.ShapeDtypeStruct((n, quarter, quarter), jnp.bfloat16) for n in (6, 4, 2)],
        in_specs=[SMEM, VMEM, VMEM],
        out_specs=[VMEM] * 3,
        compiler_params=PARAMS,
        cost_estimate=pl.CostEstimate(flops=1, bytes_accessed=4 * 1024 * 1024, transcendentals=0),
        name="pick_blocks",
    )(lane.reshape(1), left, right)

    opposite = lane_swap(picked[2], 2)

    same = (owner_list[:, None] == owner_list[None, :]) & (block_ids[None, :] < block_ids[:, None])
    slot_index = jnp.sum(same.astype(jnp.int32), axis=1)
    turned = lax.rem(owner_list + (PLANES - FIRST_PLANE) * SEATS, owners)
    place = turned * capacity + slot_index

    outgoing = pl.pallas_call(
        sum_and_place,
        out_shape=jax.ShapeDtypeStruct((owners * capacity, rows, quarter), jnp.bfloat16),
        in_specs=[SMEM, VMEM],
        out_specs=VMEM,
        compiler_params=PARAMS,
        name="sum_and_place",
    )(place, terms.reshape(LANES, blocks // 2, 2 * rows, quarter))
    outgoing = outgoing.reshape(PLANES, SEATS * capacity * rows, quarter)
    picked, opposite, outgoing = lax.optimization_barrier((picked, opposite, outgoing))
    arrived = exchange(outgoing, "own", plane_groups)
    beside, across = lane_swap(picked[0], 1), lane_swap(picked[1], 3)
    lefts, rights = pl.pallas_call(
        assemble,
        out_shape=[jax.ShapeDtypeStruct((width, width), jnp.bfloat16)] * 2,
        in_specs=[SMEM] + [VMEM] * 5,
        out_specs=[VMEM] * 2,
        compiler_params=PARAMS,
        name="assemble",
    )(lane.reshape(1), left, right, beside, across, opposite)
    lefts, rights, arrived = lax.optimization_barrier((lefts, rights, arrived))

    tile = capacity * rows
    copies = pl.pallas_call(
        fan_out,
        out_shape=jax.ShapeDtypeStruct((LANES, SEATS, PLANES, rows, quarter), jnp.bfloat16),
        in_specs=[VMEM],
        out_specs=VMEM,
        compiler_params=PARAMS,
        name="fan_out",
    )(arrived.reshape(PLANES, SEATS, capacity, rows, quarter))
    members = LANES * SEATS
    pieces = exchange(copies.reshape(members, PLANES * rows, quarter), ("dp", "own"), flat_groups)
    pieces = pieces.reshape(LANES, SEATS, PLANES // 2, 2 * rows, quarter)

    grads, product, grams = pl.pallas_call(
        precondition,
        out_shape=(
            jax.ShapeDtypeStruct((width, width), jnp.bfloat16),
            jax.ShapeDtypeStruct((members // 2, PLANES // 2, tile, quarter), jnp.bfloat16),
            jax.ShapeDtypeStruct((2, quarter, width), jnp.bfloat16),
        ),
        in_specs=[SMEM, VMEM, VMEM, VMEM],
        out_specs=(VMEM, VMEM, VMEM),
        compiler_params=PARAMS,
        name="precondition",
    )(lane.reshape(1), pieces, lefts, rights)
    product = exchange(
        product.reshape(members // 2, PLANES // 2 * tile, quarter), ("dp", "own"), half_groups
    )

    scaled = pl.pallas_call(
        regroup,
        out_shape=jax.ShapeDtypeStruct((PLANES, SEATS, tile, quarter), jnp.bfloat16),
        in_specs=[VMEM],
        out_specs=VMEM,
        compiler_params=PARAMS,
        name="regroup",
    )(product.reshape(members // 2, PLANES // 2, tile, quarter))
    grads, grams, scaled = lax.optimization_barrier((grads, grams, scaled))
    returned = exchange(scaled.reshape(PLANES, SEATS * tile, quarter), "own", plane_groups)

    used = jnp.sum((owner_list == lax.axis_index("own")).astype(jnp.int32))
    new_left, new_right = pl.pallas_call(
        statistics,
        out_shape=(
            jax.ShapeDtypeStruct(left_stat.shape, jnp.float32),
            jax.ShapeDtypeStruct(right_stat.shape, jnp.float32),
        ),
        in_specs=[SMEM, VMEM, VMEM, HBM, HBM],
        out_specs=(HBM, HBM),
        scratch_shapes=[
            pltpu.VMEM((2, 2, quarter, width), jnp.float32),
            pltpu.VMEM((2, 2, quarter, width), jnp.float32),
            pltpu.SemaphoreType.DMA((2, 2, 2)),
        ],
        compiler_params=PARAMS,
        cost_estimate=pl.CostEstimate(flops=1, bytes_accessed=1, transcendentals=0),
        name="statistics",
    )(jnp.stack([lane, used]), grads, lane_swap(grams, 1), left_stat, right_stat)

    update = pl.pallas_call(
        take_cells,
        out_shape=jax.ShapeDtypeStruct((blocks, rows, quarter), jnp.bfloat16),
        in_specs=[SMEM, VMEM],
        out_specs=HBM,
        scratch_shapes=[
            pltpu.VMEM((blocks, rows, quarter), jnp.bfloat16),
            pltpu.SemaphoreType.DMA((2,)),
        ],
        compiler_params=PARAMS,
        name="take_cells",
    )(place, returned.reshape(owners * capacity, rows, quarter))
    return (new_left, new_right, update)


def solution(mesh):
    in_specs = (
        P("dp", None, "own", None),
        P(),
        P("own", "dp", None),
        P("own", "dp", None),
        P("own", "dp", None),
        P("own", "dp", None),
    )
    out_specs = (P("own", "dp", None), P("own", "dp", None), P(None, "own", "dp"))
    return jax.shard_map(body, mesh=mesh, in_specs=in_specs, out_specs=out_specs, check_vma=False)
```

```python
import jax
import jax.numpy as jnp
from jax import lax
from jax.experimental import pallas as pl
from jax.experimental.pallas import tpu as pltpu
from jax.sharding import PartitionSpec as P

decay_rate = 0.95
epsilon = 1e-06

VMEM = pl.BlockSpec(memory_space=pltpu.VMEM)
SMEM = pl.BlockSpec(memory_space=pltpu.SMEM)
HBM = pl.BlockSpec(memory_space=pltpu.HBM)
PARAMS = pltpu.CompilerParams(vmem_limit_bytes=40 * 1024 * 1024)

PLANES, COLUMNS, CORES, LANES = 16, 4, 2, 4
LANE_ORDER = (2, 3, 0, 1)
COLUMN_ORDER = (2, 3, 0, 1)
FIRST_PLANE = 11
PLANE_ORDER = tuple((FIRST_PLANE + i) % PLANES for i in range(PLANES))
SEATS = COLUMNS * CORES
SEAT_ORDER = tuple(y * CORES + c for y in COLUMN_ORDER for c in range(CORES))


def split_columns(x_hbm, out_hbm, x, out, in_sems, out_sems):
    quarter = out.shape[3]
    parts = in_sems.shape[0]
    size = x.shape[0] // parts
    arriving, leaving = [], []
    for part in range(parts):
        blocks = pl.ds(part * size, size)
        arriving.append(pltpu.make_async_copy(x_hbm.at[blocks], x.at[blocks], in_sems.at[part]))
        leaving.append(
            pltpu.make_async_copy(out.at[:, blocks], out_hbm.at[:, blocks], out_sems.at[part])
        )
        arriving[part].start()
    for part in range(parts):
        arriving[part].wait()
        blocks = pl.ds(part * size, size)
        for place, lane in enumerate(LANE_ORDER):
            out[place, blocks] = x[blocks, :, lane * quarter : (lane + 1) * quarter]
        leaving[part].start()
    for copy in leaving:
        copy.wait()


def sum_and_place(cell_ref, terms_ref, out_hbm, out_ref, sems):
    out_ref[...] = jnp.zeros_like(out_ref)

    def step(pair, carry):
        total = terms_ref[0, pair].astype(jnp.float32)
        for term in range(1, terms_ref.shape[0]):
            total += terms_ref[term, pair].astype(jnp.float32)
        out_ref[cell_ref[2 * pair]] = total[:4].astype(out_ref.dtype)
        out_ref[cell_ref[2 * pair + 1]] = total[4:].astype(out_ref.dtype)
        return carry

    lax.fori_loop(0, terms_ref.shape[1], step, 0, unroll=64)
    parts = sems.shape[0]
    size = out_ref.shape[0] // parts
    copies = []
    for part in range(parts):
        cells = pl.ds(part * size, size)
        copies.append(pltpu.make_async_copy(out_ref.at[cells], out_hbm.at[cells], sems.at[part]))
        copies[part].start()
    for copy in copies:
        copy.wait()


def take_cells(cell_ref, cells_ref, out_hbm, out, sems):
    parts = sems.shape[0]
    size = out.shape[0] // parts

    def step(block, carry):
        out[block] = cells_ref[cell_ref[block]]
        return carry

    copies = []
    for part in range(parts):
        blocks = pl.ds(part * size, size)
        lax.fori_loop(part * size, (part + 1) * size, step, 0, unroll=32)
        copy = pltpu.make_async_copy(out.at[blocks], out_hbm.at[blocks], sems.at[part])
        copy.start()
        copies.append(copy)
    for copy in copies:
        copy.wait()


def fan_out(x_ref, out_ref):
    for i, seat in enumerate(SEAT_ORDER):
        for k, plane in enumerate(PLANE_ORDER):
            for slot in range(2):
                value = x_ref[k, seat, slot]
                for place, lane in enumerate(LANE_ORDER):
                    if lane % 2 == slot:
                        out_ref[place, i, plane] = value


def paired(first, second):
    upper = lax.broadcasted_iota(jnp.int32, first.shape, first.ndim - 2) < 4
    return (
        jnp.where(upper, first, pltpu.roll(second, 4, first.ndim - 2)),
        jnp.where(upper, pltpu.roll(first, 4, first.ndim - 2), second),
    )


def gram_rows(block, side, near):
    rows = block[near, :] if side == 0 else block[:, near]
    dims = ((1 - side,), (1 - side,))
    return lax.dot_general(rows, block[...], (dims, ((), ())), preferred_element_type=jnp.float32)


def pick_blocks(lane_ref, left_ref, right_ref, beside_ref, across_ref, opposite_ref):
    lane = lane_ref[0]
    parity = lax.rem(lane, 2)
    quarter = left_ref.shape[1]

    def block(ref, slot, lane_of_columns):
        columns = pl.ds(pl.multiple_of(lane_of_columns * quarter, quarter), quarter)
        return ref[slot, :, columns]

    for side, ref in enumerate((left_ref, right_ref)):
        for i, column in enumerate((lane, lane ^ 3, lane ^ 2)):
            beside_ref[3 * side + i] = block(ref, 1 - parity, column)
        for i, column in enumerate((lane, lane ^ 1)):
            across_ref[2 * side + i] = block(ref, 1 - parity, column)
        opposite_ref[side] = block(ref, parity, lane)


def assemble(lane_ref, own_left_ref, own_right_ref, beside, across, opposite, lefts, rights):
    lane = lane_ref[0]
    parity = lax.rem(lane, 2)
    quarter = own_left_ref.shape[1]

    def rows_of(x):
        return pl.ds(pl.multiple_of(x * quarter, quarter), quarter)

    beyond, far, last = lane ^ 1, lane ^ 3, lane ^ 2
    turn = lane & 2

    for side, (own, target, mask) in enumerate(
        ((own_left_ref, lefts, 0), (own_right_ref, rights, turn))
    ):

        def put(row, column, block):
            target[rows_of(row), rows_of(column ^ mask)] = block
            if row is not column:
                target[rows_of(column), rows_of(row ^ mask)] = block.T

        put(lane, lane, own[parity, :, rows_of(lane)])
        for other in (beyond, far, last):
            put(lane, other, own[parity, :, rows_of(other)])
        put(beyond, beyond, beside[3 * side])
        put(beyond, last, beside[3 * side + 1])
        put(beyond, far, beside[3 * side + 2])
        put(far, far, across[2 * side])
        put(far, last, across[2 * side + 1])
        put(last, last, opposite[side])


def precondition(lane_ref, pieces, left_ref, right_ref, grads_ref, out_ref, grams_ref):
    lane = lane_ref[0]
    width = grads_ref.shape[0]
    quarter = width // LANES

    def rows_of(x):
        return pl.ds(pl.multiple_of(x * quarter, quarter), quarter)

    square = jnp.zeros((1, 1), jnp.float32)
    for i, source in enumerate(LANE_ORDER):
        even, odd = [None] * COLUMNS, [None] * COLUMNS
        for j, y in enumerate(COLUMN_ORDER):
            even[y], odd[y] = paired(
                pieces[i, j * CORES].astype(jnp.float32),
                pieces[i, j * CORES + 1].astype(jnp.float32),
            )
        value = jnp.stack([jnp.stack(even, axis=1), jnp.stack(odd, axis=1)], axis=1)
        value = value.reshape(width // 8, 8, quarter)
        sums = jnp.sum(value * value, axis=0)
        square += jnp.sum(sums, axis=(0, 1), keepdims=True)
        flat = value.reshape(width, quarter).astype(jnp.bfloat16)
        grads_ref[:, source * quarter : (source + 1) * quarter] = flat
    half = jnp.dot(left_ref[...], grads_ref[...], preferred_element_type=jnp.float32)
    product = jnp.dot(
        half.astype(jnp.bfloat16), right_ref[...], preferred_element_type=jnp.float32
    )
    prod_sq = jnp.sum(jnp.sum(product * product, axis=0, keepdims=True), axis=1, keepdims=True)
    cells = float(width * width)
    ratio = jnp.sqrt(square / cells) / jnp.sqrt(prod_sq / cells + epsilon)
    pairs = out_ref.shape[1]
    for i in range(2):
        block = product[:, i * quarter : (i + 1) * quarter] * ratio
        block = block.reshape(pairs, 2, COLUMNS, 8, quarter)
        for j, y in enumerate(COLUMN_ORDER):
            for core, value in enumerate(paired(block[:, 0, y], block[:, 1, y])):
                out_ref[i * SEATS + j * CORES + core] = value.astype(out_ref.dtype)
    for side in range(2):
        grams_ref[side] = gram_rows(grads_ref, side, rows_of(lane ^ 1)).astype(grams_ref.dtype)


def regroup(x_ref, out_ref):
    for j, seat in enumerate(SEAT_ORDER):
        tiles = [x_ref[slot * SEATS + j].astype(jnp.float32) for slot in range(2)]
        for odd, value in enumerate(paired(*tiles)):
            for p in range(value.shape[0]):
                place = (2 * p + odd - FIRST_PLANE) % PLANES
                out_ref[place, seat] = value[p].astype(out_ref.dtype)


def statistics(
    info_ref, block, grams_ref, left_hbm, right_hbm, new_left_hbm, new_right_hbm, old, new, sems
):
    lane, used = info_ref[0], info_ref[1]
    parity = lax.rem(lane, 2)
    slots = (parity, 1 - parity)
    width = block.shape[0]
    quarter = old.shape[2]
    loads, stores = [], []
    for i, slot in enumerate(slots):
        for side, (src, target) in enumerate(((left_hbm, new_left_hbm), (right_hbm, new_right_hbm))):
            loads.append(pltpu.make_async_copy(src.at[slot], old.at[i, side], sems.at[0, i, side]))
            stores.append(pltpu.make_async_copy(new.at[i, side], target.at[slot], sems.at[1, i, side]))
    for copy in loads:
        copy.start()
    mine = pl.ds(pl.multiple_of(lane * quarter, quarter), quarter)
    for i, slot in enumerate(slots):
        for side in range(2):
            if i == 0:
                gram = gram_rows(block, side, mine)
            else:
                gram = grams_ref[side].astype(jnp.float32)
            loads[2 * i + side].wait()
            was = old[i, side]
            new[i, side] = jnp.where(slot < used, decay_rate * was + gram / width, was)
            stores[2 * i + side].start()
    for copy in stores:
        copy.wait()


def lane_swap(x, mask):
    return lax.ppermute(x, "dp", [(i, i ^ mask) for i in range(LANES)])


def exchange(x, axes, groups):
    return lax.all_to_all(
        x, axes, split_axis=0, concat_axis=0, tiled=True, axis_index_groups=groups
    )


def body(partial_grads, owner_list, left_stat, right_stat, left_root, right_root):
    owners = PLANES * SEATS
    capacity, quarter, width = left_stat.shape
    blocks = owner_list.shape[0]
    rows = width // owners
    block_ids = jnp.arange(blocks, dtype=jnp.int32)
    lane = lax.axis_index("dp")
    lane_groups = [list(LANE_ORDER)]
    plane_groups = [[z * SEATS + seat for z in PLANE_ORDER] for seat in range(SEATS)]
    flat_groups = [
        [x * owners + z * SEATS + seat for x in LANE_ORDER for seat in SEAT_ORDER]
        for z in range(PLANES)
    ]

    half_groups = [
        [x * owners + z * SEATS + seat for x in (half, half + 1) for seat in SEAT_ORDER]
        for half in (0, 2)
        for z in range(PLANES)
    ]

    terms = pl.pallas_call(
        split_columns,
        out_shape=jax.ShapeDtypeStruct((LANES, blocks, rows, quarter), jnp.bfloat16),
        in_specs=[HBM],
        out_specs=HBM,
        scratch_shapes=[
            pltpu.VMEM((blocks, rows, width), jnp.bfloat16),
            pltpu.VMEM((LANES, blocks, rows, quarter), jnp.bfloat16),
            pltpu.SemaphoreType.DMA((4,)),
            pltpu.SemaphoreType.DMA((4,)),
        ],
        name="split_columns",
    )(partial_grads[0])
    left, right, terms = lax.optimization_barrier((left_root, right_root, terms))
    terms = exchange(terms, "dp", lane_groups)
    picked = pl.pallas_call(
        pick_blocks,
        out_shape=[jax.ShapeDtypeStruct((n, quarter, quarter), jnp.bfloat16) for n in (6, 4, 2)],
        in_specs=[SMEM, VMEM, VMEM],
        out_specs=[VMEM] * 3,
        compiler_params=PARAMS,
        cost_estimate=pl.CostEstimate(flops=1, bytes_accessed=4 * 1024 * 1024, transcendentals=0),
        name="pick_blocks",
    )(lane.reshape(1), left, right)

    opposite = lane_swap(picked[2], 2)

    same = (owner_list[:, None] == owner_list[None, :]) & (block_ids[None, :] < block_ids[:, None])
    slot_index = jnp.sum(same.astype(jnp.int32), axis=1)
    turned = lax.rem(owner_list + (PLANES - FIRST_PLANE) * SEATS, owners)
    place = turned * capacity + slot_index

    outgoing = pl.pallas_call(
        sum_and_place,
        out_shape=jax.ShapeDtypeStruct((owners * capacity, rows, quarter), jnp.bfloat16),
        in_specs=[SMEM, VMEM],
        out_specs=HBM,
        scratch_shapes=[
            pltpu.VMEM((owners * capacity, rows, quarter), jnp.bfloat16),
            pltpu.SemaphoreType.DMA((2,)),
        ],
        compiler_params=PARAMS,
        name="sum_and_place",
    )(place, terms.reshape(LANES, blocks // 2, 2 * rows, quarter))
    outgoing = outgoing.reshape(PLANES, SEATS * capacity * rows, quarter)
    picked, opposite, outgoing = lax.optimization_barrier((picked, opposite, outgoing))
    arrived = exchange(outgoing, "own", plane_groups)
    beside, across = lane_swap(picked[0], 1), lane_swap(picked[1], 3)
    lefts, rights = pl.pallas_call(
        assemble,
        out_shape=[jax.ShapeDtypeStruct((width, width), jnp.bfloat16)] * 2,
        in_specs=[SMEM] + [VMEM] * 5,
        out_specs=[VMEM] * 2,
        compiler_params=PARAMS,
        name="assemble",
    )(lane.reshape(1), left, right, beside, across, opposite)
    lefts, rights, arrived = lax.optimization_barrier((lefts, rights, arrived))

    tile = capacity * rows
    copies = pl.pallas_call(
        fan_out,
        out_shape=jax.ShapeDtypeStruct((LANES, SEATS, PLANES, rows, quarter), jnp.bfloat16),
        in_specs=[VMEM],
        out_specs=VMEM,
        compiler_params=PARAMS,
        name="fan_out",
    )(arrived.reshape(PLANES, SEATS, capacity, rows, quarter))
    members = LANES * SEATS
    pieces = exchange(copies.reshape(members, PLANES * rows, quarter), ("dp", "own"), flat_groups)
    pieces = pieces.reshape(LANES, SEATS, PLANES // 2, 2 * rows, quarter)

    grads, product, grams = pl.pallas_call(
        precondition,
        out_shape=(
            jax.ShapeDtypeStruct((width, width), jnp.bfloat16),
            jax.ShapeDtypeStruct((members // 2, PLANES // 2, tile, quarter), jnp.bfloat16),
            jax.ShapeDtypeStruct((2, quarter, width), jnp.bfloat16),
        ),
        in_specs=[SMEM, VMEM, VMEM, VMEM],
        out_specs=(VMEM, VMEM, VMEM),
        compiler_params=PARAMS,
        name="precondition",
    )(lane.reshape(1), pieces, lefts, rights)
    product = exchange(
        product.reshape(members // 2, PLANES // 2 * tile, quarter), ("dp", "own"), half_groups
    )

    scaled = pl.pallas_call(
        regroup,
        out_shape=jax.ShapeDtypeStruct((PLANES, SEATS, tile, quarter), jnp.bfloat16),
        in_specs=[VMEM],
        out_specs=VMEM,
        compiler_params=PARAMS,
        name="regroup",
    )(product.reshape(members // 2, PLANES // 2, tile, quarter))
    grads, grams, scaled = lax.optimization_barrier((grads, grams, scaled))
    returned = exchange(scaled.reshape(PLANES, SEATS * tile, quarter), "own", plane_groups)

    used = jnp.sum((owner_list == lax.axis_index("own")).astype(jnp.int32))
    new_left, new_right = pl.pallas_call(
        statistics,
        out_shape=(
            jax.ShapeDtypeStruct(left_stat.shape, jnp.float32),
            jax.ShapeDtypeStruct(right_stat.shape, jnp.float32),
        ),
        in_specs=[SMEM, VMEM, VMEM, HBM, HBM],
        out_specs=(HBM, HBM),
        scratch_shapes=[
            pltpu.VMEM((2, 2, quarter, width), jnp.float32),
            pltpu.VMEM((2, 2, quarter, width), jnp.float32),
            pltpu.SemaphoreType.DMA((2, 2, 2)),
        ],
        compiler_params=PARAMS,
        cost_estimate=pl.CostEstimate(flops=1, bytes_accessed=1, transcendentals=0),
        name="statistics",
    )(jnp.stack([lane, used]), grads, lane_swap(grams, 1), left_stat, right_stat)

    update = pl.pallas_call(
        take_cells,
        out_shape=jax.ShapeDtypeStruct((blocks, rows, quarter), jnp.bfloat16),
        in_specs=[SMEM, VMEM],
        out_specs=HBM,
        scratch_shapes=[
            pltpu.VMEM((blocks, rows, quarter), jnp.bfloat16),
            pltpu.SemaphoreType.DMA((2,)),
        ],
        compiler_params=PARAMS,
        name="take_cells",
    )(place, returned.reshape(owners * capacity, rows, quarter))
    return (new_left, new_right, update)


def solution(mesh):
    in_specs = (
        P("dp", None, "own", None),
        P(),
        P("own", "dp", None),
        P("own", "dp", None),
        P("own", "dp", None),
        P("own", "dp", None),
    )
    out_specs = (P("own", "dp", None), P("own", "dp", None), P(None, "own", "dp"))
    return jax.shard_map(body, mesh=mesh, in_specs=in_specs, out_specs=out_specs, check_vma=False)
```
